128 devices in a mesh: group: 8 (over x, core), block: 16 (over z, y).
Axes of the slice: x: 4, y: 4, z: 4, core: 2. Of those that a mesh axis runs over, the one named last changes fastest.
Arguments:
- embeddings: bfloat16 [131072, 1024], P(('group', 'block'))
- target: int32 [131072], P(('group', 'block')), may hold values from 0 to 131071, as said below
- cluster_labels: int32 [131072], P('group'), may hold values from 0 to 65535, as said below
Outputs:
- best_cosine: float32 [131072], P(('group', 'block'))
The draws below stay inside these ranges and needn't reach their ends.
Inputs may be any that keep to these rules, and one draw needn't show every extreme that they name: target is a permutation. Number the devices group-major as d = group index * 16 + block index and let document i be the j-th of device d; then target[i] // 1024 runs over every device exactly 8 times among device d's documents, and target[i] % 1024 // 8 == d. `cluster_labels`: within each cluster group's 16384 rows the labels never fall; the labels of group g lie in [g * 8192, (g + 1) * 8192); every cluster is a contiguous run of 2 to 2048 rows inside one group, and each group has a cluster of exactly 2048 rows; different groups share no label.
All inputs are finite; a program needn't handle non-finite values.
Results may differ from the reference program's by a relative error of at most 0.00076.
Values may be sent and summed in bfloat16 or wider, within the bound.
A program may use at most 64 MiB of HBM per device.

```python
import jax
import jax.numpy as jnp
from jax import lax

E = 1024
DOC_DEV = 1024
DOCS = 131072
SLOT = 8
GROUP_ROWS = 16384
MOST = 2048
CAND = 8192
N_GROUP = 8
N_BLOCK = 16
DEVICES = 128


def layout(key):
    perm_key, label_key = jax.random.split(key)
    ranks = jax.vmap(lambda k: jax.random.permutation(k, DOC_DEV))(jax.random.split(perm_key, DEVICES))
    source = jnp.arange(DEVICES, dtype=jnp.int32)[:, None]
    target = ranks // SLOT * DOC_DEV + source * SLOT + ranks % SLOT

    def one_group(group_key, group_id):
        keys_list = jax.random.split(group_key, 6)
        start_block = jax.random.randint(keys_list[0], (), 0, N_BLOCK - 2).astype(jnp.int32)
        lead_offset = (2 * jax.random.randint(keys_list[1], (), 3 * DOC_DEV // 8, 7 * DOC_DEV // 16 + 1)).astype(jnp.int32)
        lead_rows = start_block * DOC_DEV + lead_offset
        half_count = CAND // 2
        sizes_a = 2 * jax.random.randint(keys_list[2], (half_count - 1,), DOC_DEV // 8, MOST // 2 + 1)
        ends_a = jnp.minimum(jnp.cumsum(sizes_a), lead_rows)
        sizes_b = 2 * jax.random.randint(keys_list[3], (half_count,), DOC_DEV // 8, MOST // 2 + 1)
        ends_b = jnp.minimum(lead_rows + MOST + jnp.cumsum(sizes_b), GROUP_ROWS)
        ends = jnp.concatenate([ends_a, (lead_rows + MOST)[None], ends_b]).astype(jnp.int32)
        local = jnp.searchsorted(ends, jnp.arange(GROUP_ROWS, dtype=jnp.int32), side='right').astype(jnp.int32)
        lift = jnp.where(group_id == N_GROUP - 1, CAND - 1 - local[-1], 0).astype(jnp.int32)
        labels = (local + lift + group_id * CAND).astype(jnp.int32)
        query_start = lead_rows + jax.random.randint(keys_list[4], (), 0, DOC_DEV - lead_offset - 7)
        partner_start = (start_block + 2) * DOC_DEV + lead_offset - 8 - jax.random.randint(keys_list[5], (), 0, DOC_DEV // 16 + 1)
        base_row = group_id * GROUP_ROWS
        return (labels, (query_start + base_row).astype(jnp.int32), (partner_start + base_row).astype(jnp.int32))
    labels, firsts, seconds = jax.vmap(one_group)(jax.random.split(label_key, N_GROUP), jnp.arange(N_GROUP, dtype=jnp.int32))
    return (target.reshape(-1).astype(jnp.int32), labels.reshape(-1), firsts, seconds)


def draw_target(key, part):
    return layout(key)[0]


def draw_cluster_labels(key, part):
    return layout(key)[1]


def draw_embeddings(key, part):
    target, labels, firsts, seconds = layout(key)
    key = jax.random.fold_in(key, 7)
    center_key = jax.random.fold_in(key, 0)
    weight_key = jax.random.fold_in(key, 1)
    noise_key = jax.random.fold_in(key, 2)
    copy_key = jax.random.fold_in(key, 5)
    offsets = jnp.arange(8, dtype=jnp.int32)
    first_rows = (firsts[:, None] + offsets[None, :]).reshape(-1)
    second_rows = (seconds[:, None] + offsets[None, :]).reshape(-1)
    centers = jax.vmap(lambda lab: jax.random.normal(jax.random.fold_in(center_key, lab), (E,), jnp.float32))(labels)
    weights = jnp.exp(jax.random.uniform(weight_key, (DOCS, 1), jnp.float32, jnp.log(0.2), jnp.log(4.0)))
    weights = weights.at[first_rows].set(0.2).at[second_rows].set(0.2)
    noise = jax.random.normal(noise_key, (DOCS, E), jnp.float32)
    base = weights * centers + noise
    copy_noise = 0.02 * jax.random.normal(copy_key, (first_rows.shape[0], E), jnp.float32)
    base = base.at[second_rows].set(base[first_rows] + copy_noise)
    values = base[target]
    return values.astype(jnp.bfloat16)


def setup_inputs(seed: int = 0) -> dict:
    key_list = jax.random.split(jax.random.key(seed), 4)
    embeddings = draw_embeddings(jax.random.fold_in(key_list[3], 71), 0)
    target = draw_target(jax.random.fold_in(key_list[3], 71), 0)
    cluster_labels = draw_cluster_labels(jax.random.fold_in(key_list[3], 71), 0)
    return dict(embeddings=embeddings, target=target, cluster_labels=cluster_labels)


def reference(embeddings, target, cluster_labels):
    values = embeddings.astype(jnp.float32)
    squares = lax.optimization_barrier(jnp.sum(values * values, axis=1, keepdims=True))
    unit = (values * lax.rsqrt(squares + 1e-06)).astype(jnp.bfloat16)
    total = unit.shape[0]
    ordered = jnp.zeros_like(unit).at[target].set(unit)
    ordered_wide = ordered.astype(jnp.float32)
    window = 5 * DOC_DEV

    def block_score(block_id):
        start = (block_id * DOC_DEV).astype(jnp.int32)
        queries = lax.dynamic_slice_in_dim(ordered_wide, start, DOC_DEV, 0)
        query_labels = lax.dynamic_slice_in_dim(cluster_labels, start, DOC_DEV, 0)
        key_start = jnp.clip(start - 2 * DOC_DEV, 0, total - window).astype(jnp.int32)
        keys = lax.dynamic_slice_in_dim(ordered_wide, key_start, window, 0)
        key_labels = lax.dynamic_slice_in_dim(cluster_labels, key_start, window, 0)
        gram = lax.dot_general(queries, keys, (((1,), (1,)), ((), ())), precision=lax.Precision.HIGHEST, preferred_element_type=jnp.float32)
        query_rows = start + jnp.arange(DOC_DEV, dtype=jnp.int32)
        key_rows = key_start + jnp.arange(window, dtype=jnp.int32)
        same = (query_labels[:, None] == key_labels[None, :]) & (query_rows[:, None] != key_rows[None, :])
        return lax.optimization_barrier(jnp.max(jnp.where(same, gram, jnp.float32(-2.0)), axis=1))
    row_best = lax.map(block_score, jnp.arange(total // DOC_DEV, dtype=jnp.int32)).reshape(-1)
    return row_best[target]
```

```python
import jax
import jax.numpy as jnp
from jax import lax
from jax.experimental import pallas as pl
from jax.experimental.pallas import tpu as pltpu
from jax.sharding import PartitionSpec as P

MESH = pl.DeviceIdType.MESH


def exchange_kernel(src, dst, send_sem, recv_sem, own_sem):
    blocks = lax.axis_size("block")
    devices = lax.axis_size("group") * blocks
    me = lax.axis_index("group") * blocks + lax.axis_index("block")
    barrier = pltpu.get_barrier_semaphore()

    def greet(j, _):
        peer = lax.rem(me + j, devices)
        pl.semaphore_signal(
            barrier, inc=1, device_id=(peer // blocks, lax.rem(peer, blocks)), device_id_type=MESH
        )
        return 0

    lax.fori_loop(1, devices, greet, 0)
    pl.semaphore_wait(barrier, devices - 1)
    own = pltpu.make_async_copy(src.at[me], dst.at[me], own_sem)
    own.start()

    def send(j, _):
        peer = lax.rem(me + j, devices)
        pltpu.make_async_remote_copy(
            src.at[peer],
            dst.at[me],
            send_sem,
            recv_sem,
            device_id=(peer // blocks, lax.rem(peer, blocks)),
            device_id_type=MESH,
        ).start()
        return 0

    lax.fori_loop(1, devices, send, 0)
    own.wait()
    part = src.at[pl.ds(0, devices - 1)]
    pltpu.make_async_copy(part, part, send_sem).wait()
    pltpu.make_async_copy(part, part, recv_sem).wait()


def exchange(x, collective_id):
    return pl.pallas_call(
        exchange_kernel,
        out_shape=jax.ShapeDtypeStruct(x.shape, x.dtype),
        in_specs=[pl.BlockSpec(memory_space=pltpu.VMEM)],
        out_specs=pl.BlockSpec(memory_space=pltpu.VMEM),
        scratch_shapes=[pltpu.SemaphoreType.DMA] * 3,
        compiler_params=pltpu.CompilerParams(
            collective_id=collective_id, has_side_effects=True, vmem_limit_bytes=32 * 2**20
        ),
    )(x)


def passed_along(x, axis, by):
    length = lax.axis_size(axis)
    pairs = [(i, i + by) for i in range(length) if 0 <= i + by < length]
    return lax.ppermute(x, axis, pairs)


def body(embeddings, target, cluster_labels):
    rows = embeddings.shape[0]
    groups = lax.axis_size("group")
    blocks = lax.axis_size("block")
    devices = groups * blocks
    slot = rows // devices
    block_id = lax.axis_index("block")
    values = embeddings.astype(jnp.float32)
    squares = jnp.sum(values * values, axis=1, keepdims=True)
    unit = (values * lax.rsqrt(squares + 1e-06)).astype(jnp.bfloat16)
    position = target // rows * slot + target % slot
    outgoing = jnp.zeros_like(unit).at[position].set(unit)
    received = exchange(outgoing.reshape(devices, slot, -1), 0).reshape(rows, -1)
    own_start = block_id * rows
    own_labels = lax.dynamic_slice_in_dim(cluster_labels, own_start, rows, 0)
    own_rows = own_start + jnp.arange(rows, dtype=jnp.int32)

    def masked_gram(piece, start):
        count = piece.shape[0]
        piece_labels = lax.dynamic_slice_in_dim(cluster_labels, start, count, 0)
        gram = lax.dot_general(
            received, piece, (((1,), (1,)), ((), ())), preferred_element_type=jnp.float32
        )
        piece_rows = start + jnp.arange(count, dtype=jnp.int32)
        same = (own_labels[:, None] == piece_labels[None, :]) & (
            own_rows[:, None] != piece_rows[None, :]
        )
        return jnp.where(same, gram, jnp.float32(-2.0))

    def correlations(piece, start):
        count = piece.shape[0]
        piece_labels = lax.dynamic_slice_in_dim(cluster_labels, start, count, 0)
        return (piece_labels[0] <= own_labels[-1]) & (piece_labels[-1] >= own_labels[0])

    def add_tile(best, piece, start, valid):
        needed = valid & correlations(piece, start)

        def compute(current):
            return jnp.maximum(current, jnp.max(masked_gram(piece, start), axis=1))

        return lax.cond(needed, compute, lambda current: current, best)

    initial = jnp.full((rows,), -2.0, jnp.float32)
    row_best = add_tile(initial, received, own_start, jnp.bool_(True))
    for offset in (1, -1, 2, -2):
        other = passed_along(received, "block", offset)
        source = block_id - offset
        valid = (source >= 0) & (source < blocks)
        start = jnp.clip(source, 0, blocks - 1) * rows
        row_best = add_tile(row_best, other, start, valid)
    chunks = jnp.broadcast_to(row_best.reshape(groups, 1, 1, -1), (groups, blocks, 1, rows // groups))
    returned = exchange(chunks.reshape(devices, 1, rows // groups), 1)
    mine = lax.dynamic_slice_in_dim(returned[:, 0], block_id * slot, slot, 1)
    return mine.reshape(rows)[position]


def solution(mesh):
    return jax.shard_map(
        body,
        mesh=mesh,
        in_specs=(P(("group", "block"), None), P(("group", "block")), P("group")),
        out_specs=P(("group", "block")),
        check_vma=False,
    )
```

```python
import jax
import jax.numpy as jnp
from jax import lax
from jax.experimental import pallas as pl
from jax.experimental.pallas import tpu as pltpu
from jax.sharding import PartitionSpec as P

MESH = pl.DeviceIdType.MESH
E = 1024
ROWS = 1024
GROUPS = 8
BLOCKS = 16
DEVICES = GROUPS * BLOCKS
SLOT = ROWS // DEVICES
PIECE = ROWS // GROUPS
LOW = -2.0


def home_device(target):
    block = target // ROWS
    group, place = block // BLOCKS, block % BLOCKS
    x, half = group // 2, group % 2
    p, core = place // 2, place % 2
    turn, y = p // 4, p % 4
    y = jnp.where(turn == 1, 3 - y, y)
    return (2 * x + core) * BLOCKS + (2 * half + turn) * 4 + y


def kernel(
    emb, tgt, lab, out,
    raw, unit, outgoing, recv, own, sib, nb, lab_loc, lab_in, part_out, part_in, score, back, lanes,
    raw_sem, lab_sem, self_sem, lab_ss, lab_rs, a2a_ss, a2a_rs, sib_ss, sib_rs, nb_ss, nb_rs,
    part_ss, part_rs, back_ss, back_rs,
):
    gme = lax.axis_index("group")
    bme = lax.axis_index("block")
    me = gme * BLOCKS + bme
    core = lax.rem(gme, 2)
    sibling = gme + 1 - 2 * core
    z, y = bme // 4, lax.rem(bme, 4)
    half, turn = z // 2, lax.rem(z, 2)
    p = turn * 4 + y + turn * (3 - 2 * y)

    def at_place(q):
        q = jnp.clip(q, 0, 7)
        t, r = q // 4, lax.rem(q, 4)
        return (2 * half + t) * 4 + r + t * (3 - 2 * r)

    p_to = p - 1 + 2 * core
    p_from = p + 1 - 2 * core
    has_to = (p_to >= 0) & (p_to < 8)
    has_from = (p_from >= 0) & (p_from < 8)
    dev_to = (gme, at_place(p_to))
    dev_from = (gme, at_place(p_from))
    dev_sib = (sibling, bme)

    for t in range(GROUPS):
        part_in[0, t] = jnp.full((1, PIECE), LOW, jnp.float32)
        part_in[2, t] = jnp.full((1, PIECE), LOW, jnp.float32)
    raw_copies = []
    for i in range(4):
        rows = pl.ds(i * 256, 256)
        copy = pltpu.make_async_copy(emb.at[rows], raw.at[rows], raw_sem.at[i])
        copy.start()
        raw_copies.append(copy)
    lab_copies = []
    for i in range(4):
        place = jnp.clip(2 * p - 1 + i, 0, BLOCKS - 1)
        copy = pltpu.make_async_copy(lab.at[place], lab_loc.at[i], lab_sem.at[i])
        copy.start()
        lab_copies.append(copy)

    barrier = pltpu.get_barrier_semaphore()

    def greet(j, _):
        peer = lax.rem(me + j, DEVICES)
        pl.semaphore_signal(
            barrier, inc=1, device_id=(peer // BLOCKS, lax.rem(peer, BLOCKS)), device_id_type=MESH
        )
        return 0

    lax.fori_loop(1, DEVICES, greet, 0, unroll=False)

    for i in range(4):
        raw_copies[i].wait()
        for j in range(2):
            rows = pl.ds(i * 256 + j * 128, 128)
            values = raw[rows, :].astype(jnp.float32)
            squares = jnp.sum(values * values, axis=1, keepdims=True)
            unit[rows, :] = (values * lax.rsqrt(squares + 1e-06)).astype(jnp.bfloat16)

    target = tgt[...]
    home = home_device(target)
    position = home * SLOT + target % SLOT
    row_iota = lax.broadcasted_iota(jnp.int32, (PIECE, ROWS), 0)

    def permute(q, _):
        piece = lax.rem(gme + q, GROUPS)
        onehot = jnp.where(row_iota == position - piece * PIECE, 1.0, 0.0).astype(jnp.bfloat16)
        picked = jnp.dot(onehot, unit[...], preferred_element_type=jnp.float32)
        outgoing[pl.ds(piece * BLOCKS, BLOCKS)] = picked.reshape(BLOCKS, SLOT, E).astype(jnp.bfloat16)
        return 0

    lax.fori_loop(0, GROUPS, permute, 0, unroll=False)
    for copy in lab_copies:
        copy.wait()

    pl.semaphore_wait(barrier, DEVICES - 1)

    lab_copy = pltpu.make_async_remote_copy(
        lab_loc, lab_in, lab_ss, lab_rs, device_id=dev_sib, device_id_type=MESH
    )
    lab_copy.start()
    self_copy = pltpu.make_async_copy(outgoing.at[me], recv.at[me], self_sem)
    self_copy.start()

    def send_stage(q, _):
        to_group = lax.rem(gme + q, GROUPS)

        def send(i, _):
            to_block = lax.rem(bme + i, BLOCKS)
            pltpu.make_async_remote_copy(
                outgoing.at[to_group * BLOCKS + to_block],
                recv.at[me],
                a2a_ss,
                a2a_rs.at[q],
                device_id=(to_group, to_block),
                device_id_type=MESH,
            ).start()
            return 0

        lax.fori_loop(jnp.where(q == 0, 1, 0), BLOCKS, send, 0, unroll=False)
        return 0

    lax.fori_loop(0, GROUPS, send_stage, 0, unroll=False)

    lab_copy.wait()
    local_labels = half == core
    labels = [
        jnp.where(local_labels, lab_loc[i], lab_in[i]).astype(jnp.float32) for i in range(4)
    ]
    is0 = core == 0
    own_lab = jnp.where(is0, labels[1], labels[2])
    sib_lab = jnp.where(is0, labels[2], labels[1])
    nb_lab = jnp.where(is0, labels[3], labels[0])
    for t in range(GROUPS):
        cut = slice(t * PIECE, (t + 1) * PIECE)
        lanes[0, t] = own_lab[:, cut]
        lanes[1, t] = nb_lab[:, cut]

    def forward(piece, peer, dst, ss, rs):
        rows = pl.ds(piece * PIECE, PIECE)
        return pltpu.make_async_remote_copy(
            own.at[rows], dst.at[rows], ss, rs, device_id=peer, device_id_type=MESH
        )

    def arrive(q, _):
        piece = lax.rem(gme - q + GROUPS, GROUPS)

        @pl.when(q == 0)
        def _():
            self_copy.wait()
            part = recv.at[pl.ds(0, BLOCKS - 1)]
            pltpu.make_async_copy(part, part, a2a_rs.at[0]).wait()

        @pl.when(q > 0)
        def _():
            part = recv.at[pl.ds(0, BLOCKS)]
            pltpu.make_async_copy(part, part, a2a_rs.at[q]).wait()

        got = recv[pl.ds(piece * BLOCKS, BLOCKS)].astype(jnp.float32)
        own[pl.ds(piece * PIECE, PIECE), :] = got.reshape(PIECE, E).astype(jnp.bfloat16)

        @pl.when(has_to)
        def _():
            forward(piece, dev_to, nb, nb_ss, nb_rs.at[q]).start()

        forward(piece, dev_sib, sib, sib_ss, sib_rs).start()
        return 0

    lax.fori_loop(0, GROUPS, arrive, 0, unroll=False)

    def row_labels(which, piece):
        wide = jnp.broadcast_to(lanes[which, piece], (PIECE, PIECE))
        return wide.T

    def tile(a_rows, a_lab, b_ref, b_lab, col_best, diagonal):
        gram = lax.dot_general(
            a_rows, b_ref[...], (((1,), (1,)), ((), ())), preferred_element_type=jnp.float32
        )
        rows_best = jnp.full((PIECE, PIECE), LOW, jnp.float32)
        new = []
        for t in range(GROUPS):
            cut = slice(t * PIECE, (t + 1) * PIECE)
            same = a_lab == b_lab[:, cut]
            if diagonal is not None:
                r = lax.broadcasted_iota(jnp.int32, (PIECE, PIECE), 0) + diagonal * PIECE
                c = lax.broadcasted_iota(jnp.int32, (PIECE, PIECE), 1) + t * PIECE
                same = same & (r != c)
            masked = jnp.where(same, gram[:, cut], LOW)
            rows_best = jnp.maximum(rows_best, masked)
            new.append(jnp.max(masked.reshape(PIECE // 8, 8, PIECE), axis=0))
        return jnp.maximum(col_best, jnp.concatenate(new, axis=1)), rows_best

    def to_lanes(rows_best):
        return jnp.max(rows_best.T, axis=0, keepdims=True)

    start_best = jnp.full((8, ROWS), LOW, jnp.float32)

    def own_tile(q, best):
        rows = own[pl.ds(q * PIECE, PIECE), :]
        best, _ = tile(rows, row_labels(0, q), own, own_lab, best, q)
        return best

    own_best = lax.fori_loop(0, GROUPS, own_tile, start_best, unroll=False)

    pltpu.make_async_copy(sib, sib, sib_rs).wait()


    def near(q, bests):
        own_best, sib_best = bests
        piece = lax.rem(gme - q + GROUPS, GROUPS)
        rows = pl.ds(piece * PIECE, PIECE)

        def with_nb(own_best, sib_best):
            part = nb.at[rows]
            pltpu.make_async_copy(part, part, nb_rs.at[q]).wait()
            nb_rows, nb_labels = nb[rows, :], row_labels(1, piece)
            own_best, r2 = tile(nb_rows, nb_labels, own, own_lab, own_best, None)
            part_out[1, piece] = to_lanes(r2)

            return own_best, sib_best

        own_best, sib_best = lax.cond(has_from, with_nb, lambda a, b: (a, b), own_best, sib_best)

        def third0(sib_best):
            sib_best, r3 = tile(nb[rows, :], row_labels(1, piece), sib, sib_lab, sib_best, None)
            part_out[1, piece] = jnp.maximum(part_out[1, piece], to_lanes(r3))
            return sib_best

        def third1(sib_best):
            sib_best, r3 = tile(own[rows, :], row_labels(0, piece), sib, sib_lab, sib_best, None)
            part_in[2, piece] = to_lanes(r3)
            return sib_best

        sib_best = lax.cond(has_from & is0, third0, lambda a: a, sib_best)
        sib_best = lax.cond(core == 1, third1, lambda a: a, sib_best)
        return own_best, sib_best

    own_best, sib_best = lax.fori_loop(0, GROUPS, near, (own_best, start_best), unroll=False)

    own_line = jnp.max(own_best, axis=0, keepdims=True)
    sib_line = jnp.max(sib_best, axis=0, keepdims=True)
    for t in range(GROUPS):
        part_out[0, t] = sib_line[:, t * PIECE : (t + 1) * PIECE]

    to_sib = pltpu.make_async_remote_copy(
        part_out.at[0], part_in.at[1], part_ss.at[0], part_rs.at[0], device_id=dev_sib, device_id_type=MESH
    )
    to_nb = pltpu.make_async_remote_copy(
        part_out.at[1], part_in.at[0], part_ss.at[1], part_rs.at[1], device_id=dev_from, device_id_type=MESH
    )
    to_sib.start()

    @pl.when(has_from)
    def _():
        to_nb.start()

    to_sib.wait_recv()

    @pl.when(has_to)
    def _():
        to_nb.wait_recv()

    for t in range(GROUPS):
        best = jnp.maximum(own_line[:, t * PIECE : (t + 1) * PIECE], part_in[0, t])
        best = jnp.maximum(best, jnp.maximum(part_in[1, t], part_in[2, t]))
        score[t] = best

    own_back = pltpu.make_async_copy(score.at[gme], back.at[me], self_sem)
    own_back.start()

    def give(j, _):
        peer = lax.rem(me + j, DEVICES)
        pltpu.make_async_remote_copy(
            score.at[peer // BLOCKS],
            back.at[me],
            back_ss,
            back_rs,
            device_id=(peer // BLOCKS, lax.rem(peer, BLOCKS)),
            device_id_type=MESH,
        ).start()
        return 0

    lax.fori_loop(1, DEVICES, give, 0, unroll=False)

    part = outgoing.at[pl.ds(0, DEVICES - 1)]
    pltpu.make_async_copy(part, part, a2a_ss).wait()
    pltpu.make_async_copy(own, own, sib_ss).wait()

    @pl.when(has_to)
    def _():
        pltpu.make_async_copy(own, own, nb_ss).wait()

    to_sib.wait_send()

    @pl.when(has_from)
    def _():
        to_nb.wait_send()

    own_back.wait()
    part = back.at[pl.ds(0, DEVICES - 1)]
    pltpu.make_async_copy(part, part, back_ss).wait()
    pltpu.make_async_copy(part, part, back_rs).wait()

    by_lane = back[:, 0, :].T
    mine = jnp.zeros((SLOT, DEVICES), jnp.float32)
    for b in range(BLOCKS):
        mine = jnp.where(bme == b, by_lane[b * SLOT : (b + 1) * SLOT, :], mine)
    dev_iota = lax.broadcasted_iota(jnp.int32, (DEVICES, ROWS), 0)
    pick = jnp.where(dev_iota == home, 1.0, 0.0)
    slots = lax.dot_general(
        mine,
        pick,
        (((1,), (0,)), ((), ())),
        precision=lax.Precision.HIGHEST,
        preferred_element_type=jnp.float32,
    )
    slot_iota = lax.broadcasted_iota(jnp.int32, (SLOT, ROWS), 0)
    out[...] = jnp.sum(jnp.where(slot_iota == target % SLOT, slots, 0.0), axis=0, keepdims=True)


def body(embeddings, target, cluster_labels):
    bf, f32, i32 = jnp.bfloat16, jnp.float32, jnp.int32
    dma = pltpu.SemaphoreType.DMA
    result = pl.pallas_call(
        kernel,
        out_shape=jax.ShapeDtypeStruct((1, ROWS), f32),
        in_specs=[
            pl.BlockSpec(memory_space=pl.ANY),
            pl.BlockSpec(memory_space=pltpu.VMEM),
            pl.BlockSpec(memory_space=pl.ANY),
        ],
        out_specs=pl.BlockSpec(memory_space=pltpu.VMEM),
        scratch_shapes=[
            pltpu.VMEM((ROWS, E), bf),
            pltpu.VMEM((ROWS, E), bf),
            pltpu.VMEM((DEVICES, SLOT, E), bf),
            pltpu.VMEM((DEVICES, SLOT, E), bf),
            pltpu.VMEM((ROWS, E), bf),
            pltpu.VMEM((ROWS, E), bf),
            pltpu.VMEM((ROWS, E), bf),
            pltpu.VMEM((4, 1, ROWS), i32),
            pltpu.VMEM((4, 1, ROWS), i32),
            pltpu.VMEM((2, GROUPS, 1, PIECE), f32),
            pltpu.VMEM((3, GROUPS, 1, PIECE), f32),
            pltpu.VMEM((GROUPS, 1, PIECE), f32),
            pltpu.VMEM((DEVICES, 1, PIECE), f32),
            pltpu.VMEM((2, GROUPS, 1, PIECE), f32),
            dma((4,)),
            dma((4,)),
            dma,
            dma, dma,
            dma, dma((GROUPS,)),
            dma, dma,
            dma, dma((GROUPS,)),
            dma((2,)), dma((2,)),
            dma, dma,
        ],
        compiler_params=pltpu.CompilerParams(
            collective_id=0, has_side_effects=True, vmem_limit_bytes=48 * 2**20
        ),
        name="dedup_scores",
    )(embeddings, target.reshape(1, ROWS), cluster_labels.reshape(BLOCKS, 1, ROWS))
    return result.reshape(ROWS)


def solution(mesh):
    return jax.shard_map(
        body,
        mesh=mesh,
        in_specs=(P(("group", "block"), None), P(("group", "block")), P("group")),
        out_specs=P(("group", "block")),
        check_vma=False,
    )
```

```python
import jax
import jax.numpy as jnp
from jax import lax
from jax.experimental import pallas as pl
from jax.experimental.pallas import tpu as pltpu
from jax.sharding import PartitionSpec as P

MESH = pl.DeviceIdType.MESH
E = 1024
ROWS = 1024
GROUPS = 8
BLOCKS = 16
DEVICES = GROUPS * BLOCKS
SLOT = ROWS // DEVICES
LANES = 128
CHUNKS = ROWS // LANES
STAGES = 4
PIECE = ROWS // STAGES
LOW = -2.0
OWN, NEAR, SIB = 0, 1, 2
OFFSETS = (2, 1, 3, 0)


def place_of(block):
    z, y = block // 4, block % 4
    turn = z % 2
    return turn * 4 + y + turn * (3 - 2 * y)


def block_at(half, place):
    turn, r = place // 4, place % 4
    return (2 * half + turn) * 4 + r + turn * (3 - 2 * r)


def partner(block, core):
    place = place_of(block) - 1 + 2 * core
    ok = (place >= 0) & (place < 8)
    return block_at(block // 8, jnp.clip(place, 0, 7)), ok


def kernel(
    emb, tgt_hbm, lab, out,
    raw, unit, outgoing, recv, blk, tgt, lab_loc, lab_out, lab_in, lane_lab, col_lab, col_best, row_best, score, back, picks, turned,
    raw_sem, lab_sem, tgt_sem, self_sem, lab_ss, lab_rs, a2a_ss, a2a_rs, rl_ss, rl_rs, sib_ss, sib_rs,
    back_ss, back_rs,
):
    gme = lax.axis_index("group")
    bme = lax.axis_index("block")
    me = gme * BLOCKS + bme
    core = gme % 2
    gsib = gme + 1 - 2 * core
    xme, zme, yme = gme // 2, bme // 4, bme % 4
    place = place_of(bme)
    sum_me = xme + zme + yme
    half = bme // 8
    to_block, has_to = partner(bme, core)
    from_block, has_from = partner(bme, 1 - core)
    dev_sib = (gsib, bme)
    sum_from = xme + from_block // 4 + from_block % 4
    class_me = lax.rem(sum_me, 4)

    raw_copies = []
    for i in range(4):
        rows = pl.ds(i * 256, 256)
        raw_copies.append(pltpu.make_async_copy(emb.at[rows], raw.at[rows], raw_sem.at[i]))
    tgt_copy = pltpu.make_async_copy(tgt_hbm, tgt, tgt_sem)
    lab_copies = []
    for i in range(4):
        b = jnp.clip(2 * place - 1 + i, 0, BLOCKS - 1)
        lab_copies.append(pltpu.make_async_copy(lab.at[b], lab_loc.at[i], lab_sem.at[i]))
    for copy in raw_copies + [tgt_copy] + lab_copies:
        copy.start()

    barrier = pltpu.get_barrier_semaphore()

    def greet(j, _):
        peer = (me + j) % DEVICES
        pl.semaphore_signal(
            barrier, inc=1, device_id=(peer // BLOCKS, peer % BLOCKS), device_id_type=MESH
        )
        return 0

    lax.fori_loop(1, DEVICES, greet, 0, unroll=False)

    for which in range(3):
        col_best[which] = jnp.full((8, ROWS), LOW, jnp.float32)
        for t in range(CHUNKS):
            row_best[which, t] = jnp.full((1, LANES), LOW, jnp.float32)
            col_lab[which, t] = jnp.full((1, LANES), -1.0, jnp.float32)

    for i in range(4):
        raw_copies[i].wait()
        for j in range(2):
            rows = pl.ds(i * 256 + j * 128, 128)
            values = raw[rows, :].astype(jnp.float32)
            squares = jnp.sum(values * values, axis=1, keepdims=True)
            unit[rows, :] = (values * lax.rsqrt(squares + 1e-06)).astype(jnp.bfloat16)

    tgt_copy.wait()
    target = tgt[...]
    row_block = target // ROWS
    t_core = row_block % 2
    t_group = row_block // (2 * BLOCKS) * 2 + t_core
    t_half = row_block // BLOCKS % 2
    t_place = row_block % BLOCKS // 2
    home = t_group * BLOCKS + block_at(t_half, t_place)
    slot_of = target % SLOT
    position = home * SLOT + slot_of
    row_iota = lax.broadcasted_iota(jnp.int32, (LANES, ROWS), 0)

    def permute(q, _):
        piece = (gme + q) % GROUPS
        onehot = jnp.where(row_iota == position - piece * LANES, 1.0, 0.0).astype(jnp.bfloat16)
        picked = jnp.dot(onehot, unit[...], preferred_element_type=jnp.float32)
        outgoing[pl.ds(piece * BLOCKS, BLOCKS)] = picked.reshape(BLOCKS, SLOT, E).astype(jnp.bfloat16)
        return 0

    lax.fori_loop(0, GROUPS, permute, 0, unroll=False)
    t_to, t_ok = partner(home % BLOCKS, t_core)
    dev_iota = lax.broadcasted_iota(jnp.int32, (DEVICES, ROWS), 0)
    devs = (home, t_group * BLOCKS + t_to, home + (1 - 2 * t_core) * BLOCKS)
    for which in range(3):
        picks[which] = jnp.where(dev_iota == devs[which], 1.0, 0.0).astype(jnp.bfloat16)

    for copy in lab_copies:
        copy.wait()
    stored = lax.broadcasted_iota(jnp.int32, (1, ROWS), 1)
    slot_no = stored // SLOT
    s_class, s_block, s_core = slot_no // 32, slot_no % 32 // 2, slot_no % 2
    s_x = (s_class - s_block // 4 - s_block % 4 + 8) % 4
    natural = ((2 * s_x + s_core) * BLOCKS + s_block) * SLOT + stored % SLOT
    lab_all = jnp.concatenate([lab_loc[i] for i in range(4)], axis=0)
    high = lab_all // 256
    halves = jnp.concatenate([high, lab_all - 256 * high], axis=0).astype(jnp.float32).astype(jnp.bfloat16)
    moved = jnp.zeros((8, ROWS), jnp.float32)
    for t in range(CHUNKS):
        move = jnp.where(row_iota == natural - t * LANES, 1.0, 0.0).astype(jnp.bfloat16)
        moved = moved + jnp.dot(
            halves[:, t * LANES : (t + 1) * LANES], move, preferred_element_type=jnp.float32
        )
    lab_new = moved[:4] * 256.0 + moved[4:]
    for i in range(4):
        lab_out[i] = lab_new[i : i + 1]

    pl.semaphore_wait(barrier, DEVICES - 1)

    lab_copy = pltpu.make_async_remote_copy(
        lab_out, lab_in, lab_ss, lab_rs, device_id=dev_sib, device_id_type=MESH
    )
    lab_copy.start()
    pltpu.make_async_copy(outgoing.at[me], recv.at[OWN, class_me, zme, yme, core], a2a_rs.at[OWN, 0]).start()

    @pl.when(has_from)
    def _():
        pltpu.make_async_copy(
            outgoing.at[gme * BLOCKS + from_block],
            recv.at[NEAR, class_me, zme, yme, core],
            a2a_rs.at[NEAR, 2 * lax.rem(sum_from - sum_me + 4, 4)],
        ).start()

    routes = []
    for c in range(2):
        to_core = lax.rem(core + c, 2)
        sign = 2 * to_core - 1
        for dz in OFFSETS:
            for dy in OFFSETS:
                z, y = lax.rem(zme + dz, 4), lax.rem(yme + dy, 4)
                turn = lax.rem(z, 2)
                along = 1 - 2 * turn
                way = sign * along
                on_y = (y + way >= 0) & (y + way <= 3)
                on_z = (y == 3) & (way == 1)
                far_y = {0: way == 0, 1: way == -1, 2: way != 0, 3: way == 1}[dy]
                far_z = {0: turn == 2, 1: turn == 1, 2: turn != 2, 3: turn == 0}[dz]
                second = (on_y & far_y) | (on_z & far_z)
                block = z * 4 + y
                other = jnp.where(on_y, block + way, block + 4 * along)
                routes.append((c, 8 - dz - dy, block, jnp.where(second, NEAR, OWN), jnp.where(second, other, block)))

    def send_stage(q, _):
        for c, dx, home_block, which, block in routes:
            to_group = 2 * lax.rem(xme + q + dx, 4) + (core if c == 0 else 1 - core)

            def send():
                pltpu.make_async_remote_copy(
                    outgoing.at[to_group * BLOCKS + home_block],
                    recv.at[which, class_me, zme, yme, core],
                    a2a_ss,
                    a2a_rs.at[which, 2 * q + c],
                    device_id=(to_group, block),
                    device_id_type=MESH,
                ).start()

            if c == 0:
                pl.when((to_group != gme) | (block != bme))(send)
            else:
                send()
        return 0

    lax.fori_loop(0, STAGES, send_stage, 0, unroll=False)

    lab_copy.wait()
    labels = [
        jnp.where(half == core, lab_out[i], lab_in[i]) for i in range(4)
    ]
    is0 = core == 0
    sides = [
        jnp.where(is0, labels[1], labels[2]),
        jnp.where(has_from, jnp.where(is0, labels[3], labels[0]), -2.0),
        jnp.where(is0, labels[2], labels[1]),
    ]
    for which in range(3):
        for t in range(CHUNKS):
            lane_lab[which, t] = sides[which][:, t * LANES : (t + 1) * LANES]

    eight = recv.at[OWN, 0, 0]
    sixteen = recv.at[OWN, 0, pl.ds(0, 2)]
    thirty_two = recv.at[OWN, 0]

    def await_bytes(ref, sem):
        pltpu.make_async_copy(ref, ref, sem).wait()

    def hand_on(which, n, a, c, dy, dz, block):
        for step in range(2):
            yy = lax.rem(yme + step * dy + 4, 4)
            zz = lax.rem(zme + step * dz + 4, 4)

            def go(src, dst):
                pltpu.make_async_remote_copy(
                    src, dst, rl_ss.at[which], rl_rs.at[1 - which, n], device_id=(gme, block), device_id_type=MESH
                ).start()

            @pl.when(dy != 0)
            def _():
                go(recv.at[which, a, :, yy, c], recv.at[1 - which, a, :, yy, c])

            @pl.when(dy == 0)
            def _():
                go(recv.at[which, a, zz, :, c], recv.at[1 - which, a, zz, :, c])

    def own_class(q):
        return lax.rem(sum_me - q + 4, 4)

    def near_class(q):
        return lax.rem(sum_from - q + 4, 4)

    def first(q, c):
        n = 2 * q + c
        from_core = lax.rem(core + c, 2)

        @pl.when(has_to)
        def _():
            await_bytes(eight, a2a_rs.at[OWN, n])
            hand_on(OWN, n, own_class(q), from_core, yme - to_block % 4, zme - to_block // 4, to_block)

        @pl.when(jnp.logical_not(has_to))
        def _():
            await_bytes(sixteen, a2a_rs.at[OWN, n])

        @pl.when(has_from)
        def _():
            await_bytes(eight, a2a_rs.at[NEAR, n])
            hand_on(NEAR, n, near_class(q), from_core, yme - from_block % 4, zme - from_block // 4, from_block)

    def lay_out(which, x):
        got = recv[which, x].astype(jnp.float32)
        blk[which, pl.ds(x * PIECE, PIECE), :] = got.reshape(PIECE, E).astype(jnp.bfloat16)
        for c in range(2):
            col_lab[which, 2 * x + c] = lane_lab[which, 2 * x + c]

    r_iota = lax.broadcasted_iota(jnp.int32, (PIECE, LANES), 0)
    c_iota = lax.broadcasted_iota(jnp.int32, (PIECE, LANES), 1)
    ahead = r_iota - c_iota

    def product(a, x, b, same_block=False):
        gram = lax.dot_general(
            blk[a, pl.ds(x * PIECE, PIECE), :],
            blk[b],
            (((1,), (1,)), ((), ())),
            preferred_element_type=jnp.float32,
        )
        a_lab = jnp.concatenate(
            [jnp.broadcast_to(lane_lab[a, 2 * x + c], (LANES, LANES)).T for c in range(2)], axis=0
        )
        rows_best = jnp.full((PIECE, LANES), LOW, jnp.float32)
        for t in range(CHUNKS):
            cut = slice(t * LANES, (t + 1) * LANES)
            same = a_lab == col_lab[b, t]
            if same_block:
                same = same & (ahead != t * LANES - x * PIECE)
            masked = jnp.where(same, gram[:, cut], LOW)
            rows_best = jnp.maximum(rows_best, masked)
            col_best[b, :, cut] = jnp.maximum(
                col_best[b, :, cut], jnp.max(masked.reshape(PIECE // 8, 8, LANES), axis=0)
            )
        return rows_best

    def fold_rows(which, x, rows_best):
        for c in range(2):
            line = jnp.max(rows_best[c * LANES : (c + 1) * LANES].T, axis=0, keepdims=True)
            row_best[which, 2 * x + c] = jnp.maximum(row_best[which, 2 * x + c], line)

    def complete(q):
        x, w = own_class(q), near_class(q)

        @pl.when(has_to)
        def _():
            for c in range(2):
                await_bytes(eight, rl_rs.at[OWN, 2 * q + c])

        pltpu.make_async_remote_copy(
            recv.at[OWN, x], recv.at[SIB, x], sib_ss, sib_rs.at[q], device_id=dev_sib, device_id_type=MESH
        ).start()
        lay_out(OWN, x)

        @pl.when(has_from)
        def _():
            for c in range(2):
                await_bytes(eight, rl_rs.at[NEAR, 2 * q + c])
            lay_out(NEAR, w)

        own_rows = product(OWN, x, OWN, same_block=True)
        fold_rows(OWN, x, jnp.maximum(own_rows, product(OWN, x, NEAR)))
        fold_rows(NEAR, w, product(NEAR, w, OWN))

    third = 1 - core

    def sibling(q):
        x, w = own_class(q), near_class(q)
        await_bytes(thirty_two, sib_rs.at[q])
        lay_out(SIB, x)
        fold_rows(SIB, x, product(SIB, x, third))
        v = jnp.where(core == 0, w, x)
        fold_rows(third, v, product(third, v, SIB))

    def step(s, _):
        @pl.when(s < STAGES)
        def _():
            first(s, 0)
            first(s, 1)

        @pl.when((s >= 1) & (s < STAGES + 1))
        def _():
            complete(s - 1)

        @pl.when(s >= 2)
        def _():
            sibling(s - 2)

        return 0

    lax.fori_loop(0, STAGES + 2, step, 0, unroll=False)

    for which in range(3):
        for t in range(CHUNKS):
            cut = slice(t * LANES, (t + 1) * LANES)
            line = jnp.max(col_best[which, :, cut], axis=0, keepdims=True)
            score[which, t] = jnp.maximum(line, row_best[which, t])

    own_back = pltpu.make_async_copy(score.at[:, 2 * class_me + zme // 2], back.at[me], self_sem)
    own_back.start()

    near_coords = [(lax.rem(zme + dz, 4), lax.rem(yme + dy, 4)) for dz in OFFSETS for dy in OFFSETS]

    def give(i, _):
        group = lax.rem(gme + 4 + i, GROUPS)
        for n, (z, y) in enumerate(near_coords):
            chunk = 2 * lax.rem(group // 2 + z + y, 4) + z // 2

            def send():
                pltpu.make_async_remote_copy(
                    score.at[:, chunk],
                    back.at[me],
                    back_ss,
                    back_rs,
                    device_id=(group, z * 4 + y),
                    device_id_type=MESH,
                ).start()

            if n == BLOCKS - 1:
                pl.when(i != 4)(send)
            else:
                send()
        return 0

    lax.fori_loop(0, GROUPS, give, 0, unroll=False)

    await_bytes(outgoing.at[pl.ds(0, DEVICES - 2)], a2a_ss)

    @pl.when(jnp.logical_not(has_from))
    def _():
        await_bytes(outgoing.at[0], a2a_ss)

    @pl.when(has_to)
    def _():
        await_bytes(recv.at[OWN, pl.ds(0, 2)], rl_ss.at[OWN])

    @pl.when(has_from)
    def _():
        await_bytes(recv.at[OWN, pl.ds(0, 2)], rl_ss.at[NEAR])

    await_bytes(recv.at[OWN], sib_ss)
    own_back.wait()
    part = back.at[pl.ds(0, DEVICES - 1)]
    await_bytes(part, back_ss)
    await_bytes(part, back_rs)

    slot_iota = lax.broadcasted_iota(jnp.int32, (SLOT, ROWS), 0)
    best = jnp.full((SLOT, ROWS), LOW, jnp.float32)
    for which in range(3):
        turned[...] = back[:, which, 0, :].T
        rest = turned[pl.ds((lax.rem(bme, 8) * 2 + core) * SLOT, SLOT), :]
        parts = []
        for _ in range(3):
            parts.append(rest.astype(jnp.bfloat16))
            rest = rest - parts[-1].astype(jnp.float32)
        slots = jnp.zeros((SLOT, ROWS), jnp.float32)
        for part in parts:
            slots = slots + jnp.dot(part, picks[which], preferred_element_type=jnp.float32)
        if which == NEAR:
            slots = jnp.where(t_ok, slots, LOW)
        best = jnp.maximum(best, slots)
    out[...] = jnp.sum(jnp.where(slot_iota == slot_of, best, 0.0), axis=0, keepdims=True)


def body(embeddings, target, cluster_labels):
    bf, f32, i32 = jnp.bfloat16, jnp.float32, jnp.int32
    dma = pltpu.SemaphoreType.DMA
    result = pl.pallas_call(
        kernel,
        out_shape=jax.ShapeDtypeStruct((1, ROWS), f32),
        in_specs=[pl.BlockSpec(memory_space=pl.ANY)] * 3,
        out_specs=pl.BlockSpec(memory_space=pltpu.VMEM),
        scratch_shapes=[
            pltpu.VMEM((ROWS, E), bf),
            pltpu.VMEM((ROWS, E), bf),
            pltpu.VMEM((DEVICES, SLOT, E), bf),
            pltpu.VMEM((3, 4, 4, 4, 2, SLOT, E), bf),
            pltpu.VMEM((3, ROWS, E), bf),
            pltpu.VMEM((1, ROWS), i32),
            pltpu.VMEM((4, 1, ROWS), i32),
            pltpu.VMEM((4, 1, ROWS), f32),
            pltpu.VMEM((4, 1, ROWS), f32),
            pltpu.VMEM((3, CHUNKS, 1, LANES), f32),
            pltpu.VMEM((3, CHUNKS, 1, LANES), f32),
            pltpu.VMEM((3, 8, ROWS), f32),
            pltpu.VMEM((3, CHUNKS, 1, LANES), f32),
            pltpu.VMEM((3, CHUNKS, 1, LANES), f32),
            pltpu.VMEM((DEVICES, 3, 1, LANES), f32),
            pltpu.VMEM((3, DEVICES, ROWS), bf),
            pltpu.VMEM((LANES, DEVICES), f32),
            dma((4,)),
            dma((4,)),
            dma,
            dma,
            dma, dma,
            dma, dma((2, GROUPS)),
            dma((2,)), dma((2, GROUPS)),
            dma, dma((STAGES,)),
            dma, dma,
        ],
        compiler_params=pltpu.CompilerParams(
            collective_id=0, has_side_effects=True, vmem_limit_bytes=60 * 2**20
        ),
        name="dedup_scores",
    )(embeddings, target.reshape(1, ROWS), cluster_labels.reshape(BLOCKS, 1, ROWS))
    return result.reshape(ROWS)


def solution(mesh):
    return jax.shard_map(
        body,
        mesh=mesh,
        in_specs=(P(("group", "block"), None), P(("group", "block")), P("group")),
        out_specs=P(("group", "block")),
        check_vma=False,
    )
```

```python
import jax
import jax.numpy as jnp
from jax import lax
from jax.experimental import pallas as pl
from jax.experimental.pallas import tpu as pltpu
from jax.sharding import PartitionSpec as P

MESH = pl.DeviceIdType.MESH
E = 1024
ROWS = 1024
GROUPS = 8
BLOCKS = 16
DEVICES = GROUPS * BLOCKS
SLOT = ROWS // DEVICES
LANES = 128
CHUNKS = ROWS // LANES
STAGES = 4
PIECE = ROWS // STAGES
LOW = -2.0
OWN, NEAR, SIB = 0, 1, 2
OFFSETS = (2, 1, 3, 0)


def place_of(block):
    z, y = block // 4, block % 4
    turn = z % 2
    return turn * 4 + y + turn * (3 - 2 * y)


def block_at(half, place):
    turn, r = place // 4, place % 4
    return (2 * half + turn) * 4 + r + turn * (3 - 2 * r)


def partner(block, core):
    place = place_of(block) - 1 + 2 * core
    ok = (place >= 0) & (place < 8)
    return block_at(block // 8, jnp.clip(place, 0, 7)), ok


def kernel(
    emb, tgt_hbm, lab, out,
    raw, unit, outgoing, recv, blk, tgt, lab_loc, lab_out, lab_in, lane_lab, col_lab, col_best, row_best, score, back, picks, turned,
    raw_sem, lab_sem, tgt_sem, self_sem, lab_ss, lab_rs, a2a_ss, a2a_rs, rl_ss, rl_rs, sib_ss, sib_rs,
    back_ss, back_rs, row_sem,
):
    gme = lax.axis_index("group")
    bme = lax.axis_index("block")
    me = gme * BLOCKS + bme
    core = gme % 2
    gsib = gme + 1 - 2 * core
    xme, zme, yme = gme // 2, bme // 4, bme % 4
    place = place_of(bme)
    sum_me = xme + zme + yme
    half = bme // 8
    to_block, has_to = partner(bme, core)
    from_block, has_from = partner(bme, 1 - core)
    dev_sib = (gsib, bme)
    sum_from = xme + from_block // 4 + from_block % 4
    class_me = lax.rem(sum_me, 4)

    raw_copies = []
    for i in range(4):
        rows = pl.ds(i * 256, 256)
        raw_copies.append(pltpu.make_async_copy(emb.at[rows], raw.at[rows], raw_sem.at[i]))
    tgt_copy = pltpu.make_async_copy(tgt_hbm, tgt, tgt_sem)
    lab_copies = []
    for i in range(4):
        b = jnp.clip(2 * place - 1 + i, 0, BLOCKS - 1)
        lab_copies.append(pltpu.make_async_copy(lab.at[b], lab_loc.at[i], lab_sem.at[i]))
    for copy in raw_copies + [tgt_copy] + lab_copies:
        copy.start()

    barrier = pltpu.get_barrier_semaphore()

    row = [lax.rem(bme + i, BLOCKS) for i in range(1, BLOCKS)]
    column = [lax.rem(gme + i, GROUPS) for i in range(1, GROUPS)]
    for block in row:
        pl.semaphore_signal(barrier, inc=1, device_id=(gme, block), device_id_type=MESH)
    for group in column:
        pl.semaphore_signal(barrier, inc=1, device_id=(group, bme), device_id_type=MESH)

    for which in range(3):
        col_best[which] = jnp.full((8, ROWS), LOW, jnp.float32)
        for t in range(CHUNKS):
            row_best[which, t] = jnp.full((1, LANES), LOW, jnp.float32)
            col_lab[which, t] = jnp.full((1, LANES), -1.0, jnp.float32)

    for i in range(4):
        raw_copies[i].wait()
        for j in range(2):
            rows = pl.ds(i * 256 + j * 128, 128)
            values = raw[rows, :].astype(jnp.float32)
            squares = jnp.sum(values * values, axis=1, keepdims=True)
            unit[rows, :] = (values * lax.rsqrt(squares + 1e-06)).astype(jnp.bfloat16)

    tgt_copy.wait()
    target = tgt[...]
    row_block = target // ROWS
    t_core = row_block % 2
    t_group = row_block // (2 * BLOCKS) * 2 + t_core
    t_half = row_block // BLOCKS % 2
    t_place = row_block % BLOCKS // 2
    home = t_group * BLOCKS + block_at(t_half, t_place)
    slot_of = target % SLOT
    position = home * SLOT + slot_of
    row_iota = lax.broadcasted_iota(jnp.int32, (LANES, ROWS), 0)

    def permute(q, _):
        piece = (gme + q) % GROUPS
        onehot = jnp.where(row_iota == position - piece * LANES, 1.0, 0.0).astype(jnp.bfloat16)
        picked = jnp.dot(onehot, unit[...], preferred_element_type=jnp.float32)
        outgoing[pl.ds(piece * BLOCKS, BLOCKS)] = picked.reshape(BLOCKS, SLOT, E).astype(jnp.bfloat16)
        return 0

    lax.fori_loop(0, GROUPS, permute, 0, unroll=False)
    t_to, t_ok = partner(home % BLOCKS, t_core)
    dev_iota = lax.broadcasted_iota(jnp.int32, (DEVICES, ROWS), 0)
    devs = (home, t_group * BLOCKS + t_to, home + (1 - 2 * t_core) * BLOCKS)
    for which in range(3):
        picks[which] = jnp.where(dev_iota == devs[which], 1.0, 0.0).astype(jnp.bfloat16)

    for copy in lab_copies:
        copy.wait()
    stored = lax.broadcasted_iota(jnp.int32, (1, ROWS), 1)
    slot_no = stored // SLOT
    s_class, s_block, s_core = slot_no // 32, slot_no % 32 // 2, slot_no % 2
    s_x = (s_class - s_block // 4 - s_block % 4 + 8) % 4
    natural = ((2 * s_x + s_core) * BLOCKS + s_block) * SLOT + stored % SLOT
    lab_all = jnp.concatenate([lab_loc[i] for i in range(4)], axis=0)
    high = lab_all // 256
    halves = jnp.concatenate([high, lab_all - 256 * high], axis=0).astype(jnp.float32).astype(jnp.bfloat16)
    moved = jnp.zeros((8, ROWS), jnp.float32)
    for t in range(CHUNKS):
        move = jnp.where(row_iota == natural - t * LANES, 1.0, 0.0).astype(jnp.bfloat16)
        moved = moved + jnp.dot(
            halves[:, t * LANES : (t + 1) * LANES], move, preferred_element_type=jnp.float32
        )
    lab_new = moved[:4] * 256.0 + moved[4:]
    for i in range(4):
        lab_out[i] = lab_new[i : i + 1]

    pl.semaphore_wait(barrier, len(row) + len(column))
    for block in row:
        pl.semaphore_signal(row_sem, inc=1, device_id=(gme, block), device_id_type=MESH)

    lab_copy = pltpu.make_async_remote_copy(
        lab_out, lab_in, lab_ss, lab_rs, device_id=dev_sib, device_id_type=MESH
    )
    lab_copy.start()
    pltpu.make_async_copy(outgoing.at[me], recv.at[OWN, class_me, zme, yme, core], a2a_rs.at[OWN, 0]).start()

    @pl.when(has_from)
    def _():
        pltpu.make_async_copy(
            outgoing.at[gme * BLOCKS + from_block],
            recv.at[NEAR, class_me, zme, yme, core],
            a2a_rs.at[NEAR, 2 * lax.rem(sum_from - sum_me + 4, 4)],
        ).start()

    routes = []
    for c in range(2):
        to_core = lax.rem(core + c, 2)
        sign = 2 * to_core - 1
        for dz in OFFSETS:
            for dy in OFFSETS:
                z, y = lax.rem(zme + dz, 4), lax.rem(yme + dy, 4)
                turn = lax.rem(z, 2)
                along = 1 - 2 * turn
                way = sign * along
                on_y = (y + way >= 0) & (y + way <= 3)
                on_z = (y == 3) & (way == 1)
                far_y = {0: way == 0, 1: way == -1, 2: way != 0, 3: way == 1}[dy]
                far_z = {0: turn == 2, 1: turn == 1, 2: turn != 2, 3: turn == 0}[dz]
                second = (on_y & far_y) | (on_z & far_z)
                block = z * 4 + y
                other = jnp.where(on_y, block + way, block + 4 * along)
                routes.append((c, dz, dy, block, jnp.where(second, NEAR, OWN), jnp.where(second, other, block)))

    def send(q, c, x, home_block, which, block):
        to_group = 2 * x + (core if c == 0 else 1 - core)
        pltpu.make_async_remote_copy(
            outgoing.at[to_group * BLOCKS + home_block],
            recv.at[which, class_me, zme, yme, core],
            a2a_ss,
            a2a_rs.at[which, 2 * q + c],
            device_id=(to_group, block),
            device_id_type=MESH,
        ).start()

    for c, dz, dy, home_block, which, block in routes:
        if dz == 0 and dy == 0:
            for dx in OFFSETS:
                if dx or c:
                    send(dx, c, lax.rem(xme + dx, 4), home_block, which, block)
        elif c == 0:

            @pl.when(block != bme)
            def _():
                send((dz + dy) % 4, c, xme, home_block, which, block)

    pl.semaphore_wait(row_sem, len(row))

    def send_stage(q, _):
        for c, dz, dy, home_block, which, block in routes:
            if dz == 0 and dy == 0:
                continue
            dx = lax.rem(q + 8 - dz - dy, 4)

            def go():
                send(q, c, lax.rem(xme + dx, 4), home_block, which, block)

            if c == 0:
                pl.when(dx != 0)(go)
            else:
                go()
        return 0

    lax.fori_loop(0, STAGES, send_stage, 0, unroll=False)

    lab_copy.wait()
    labels = [
        jnp.where(half == core, lab_out[i], lab_in[i]) for i in range(4)
    ]
    is0 = core == 0
    sides = [
        jnp.where(is0, labels[1], labels[2]),
        jnp.where(has_from, jnp.where(is0, labels[3], labels[0]), -2.0),
        jnp.where(is0, labels[2], labels[1]),
    ]
    for which in range(3):
        for t in range(CHUNKS):
            lane_lab[which, t] = sides[which][:, t * LANES : (t + 1) * LANES]

    eight = recv.at[OWN, 0, 0]
    sixteen = recv.at[OWN, 0, pl.ds(0, 2)]
    thirty_two = recv.at[OWN, 0]

    def await_bytes(ref, sem):
        pltpu.make_async_copy(ref, ref, sem).wait()

    def hand_on(which, n, a, c, dy, dz, block):
        for step in range(2):
            yy = lax.rem(yme + step * dy + 4, 4)
            zz = lax.rem(zme + step * dz + 4, 4)

            def go(src, dst):
                pltpu.make_async_remote_copy(
                    src, dst, rl_ss.at[which], rl_rs.at[1 - which, n], device_id=(gme, block), device_id_type=MESH
                ).start()

            @pl.when(dy != 0)
            def _():
                go(recv.at[which, a, :, yy, c], recv.at[1 - which, a, :, yy, c])

            @pl.when(dy == 0)
            def _():
                go(recv.at[which, a, zz, :, c], recv.at[1 - which, a, zz, :, c])

    def own_class(q):
        return lax.rem(sum_me - q + 4, 4)

    def near_class(q):
        return lax.rem(sum_from - q + 4, 4)

    def first(q, c):
        n = 2 * q + c
        from_core = lax.rem(core + c, 2)

        @pl.when(has_to)
        def _():
            await_bytes(eight, a2a_rs.at[OWN, n])
            hand_on(OWN, n, own_class(q), from_core, yme - to_block % 4, zme - to_block // 4, to_block)

        @pl.when(jnp.logical_not(has_to))
        def _():
            await_bytes(sixteen, a2a_rs.at[OWN, n])

        @pl.when(has_from)
        def _():
            await_bytes(eight, a2a_rs.at[NEAR, n])
            hand_on(NEAR, n, near_class(q), from_core, yme - from_block % 4, zme - from_block // 4, from_block)

    def lay_out(which, x):
        got = recv[which, x].astype(jnp.float32)
        blk[which, pl.ds(x * PIECE, PIECE), :] = got.reshape(PIECE, E).astype(jnp.bfloat16)
        for c in range(2):
            col_lab[which, 2 * x + c] = lane_lab[which, 2 * x + c]

    r_iota = lax.broadcasted_iota(jnp.int32, (PIECE, LANES), 0)
    c_iota = lax.broadcasted_iota(jnp.int32, (PIECE, LANES), 1)
    ahead = r_iota - c_iota

    def product(a, x, b, same_block=False):
        gram = lax.dot_general(
            blk[a, pl.ds(x * PIECE, PIECE), :],
            blk[b],
            (((1,), (1,)), ((), ())),
            preferred_element_type=jnp.float32,
        )
        a_lab = jnp.concatenate(
            [jnp.broadcast_to(lane_lab[a, 2 * x + c], (LANES, LANES)).T for c in range(2)], axis=0
        )
        rows_best = jnp.full((PIECE, LANES), LOW, jnp.float32)
        for t in range(CHUNKS):
            cut = slice(t * LANES, (t + 1) * LANES)
            same = a_lab == col_lab[b, t]
            if same_block:
                same = same & (ahead != t * LANES - x * PIECE)
            masked = jnp.where(same, gram[:, cut], LOW)
            rows_best = jnp.maximum(rows_best, masked)
            col_best[b, :, cut] = jnp.maximum(
                col_best[b, :, cut], jnp.max(masked.reshape(PIECE // 8, 8, LANES), axis=0)
            )
        return rows_best

    def fold_rows(which, x, rows_best):
        for c in range(2):
            line = jnp.max(rows_best[c * LANES : (c + 1) * LANES].T, axis=0, keepdims=True)
            row_best[which, 2 * x + c] = jnp.maximum(row_best[which, 2 * x + c], line)

    def complete(q):
        x, w = own_class(q), near_class(q)

        @pl.when(has_to)
        def _():
            for c in range(2):
                await_bytes(eight, rl_rs.at[OWN, 2 * q + c])

        pltpu.make_async_remote_copy(
            recv.at[OWN, x], recv.at[SIB, x], sib_ss, sib_rs.at[q], device_id=dev_sib, device_id_type=MESH
        ).start()
        lay_out(OWN, x)

        @pl.when(has_from)
        def _():
            for c in range(2):
                await_bytes(eight, rl_rs.at[NEAR, 2 * q + c])
            lay_out(NEAR, w)

        own_rows = product(OWN, x, OWN, same_block=True)
        fold_rows(OWN, x, jnp.maximum(own_rows, product(OWN, x, NEAR)))
        fold_rows(NEAR, w, product(NEAR, w, OWN))

    third = 1 - core

    def sibling(q):
        x, w = own_class(q), near_class(q)
        await_bytes(thirty_two, sib_rs.at[q])
        lay_out(SIB, x)
        fold_rows(SIB, x, product(SIB, x, third))
        v = jnp.where(core == 0, w, x)
        fold_rows(third, v, product(third, v, SIB))

    def step(s, _):
        @pl.when(s < STAGES)
        def _():
            first(s, 0)
            first(s, 1)

        @pl.when(s >= 2)
        def _():
            sibling(s - 2)

        @pl.when((s >= 1) & (s < STAGES + 1))
        def _():
            complete(s - 1)

        return 0

    lax.fori_loop(0, STAGES + 2, step, 0, unroll=False)

    for which in range(3):
        for t in range(CHUNKS):
            cut = slice(t * LANES, (t + 1) * LANES)
            line = jnp.max(col_best[which, :, cut], axis=0, keepdims=True)
            score[which, t] = jnp.maximum(line, row_best[which, t])

    own_back = pltpu.make_async_copy(score.at[:, 2 * class_me + zme // 2], back.at[me], self_sem)
    own_back.start()

    near_coords = [(lax.rem(zme + dz, 4), lax.rem(yme + dy, 4)) for dz in OFFSETS for dy in OFFSETS]

    def give(i, _):
        group = lax.rem(gme + 4 + i, GROUPS)
        for n, (z, y) in enumerate(near_coords):
            chunk = 2 * lax.rem(group // 2 + z + y, 4) + z // 2

            def send():
                pltpu.make_async_remote_copy(
                    score.at[:, chunk],
                    back.at[me],
                    back_ss,
                    back_rs,
                    device_id=(group, z * 4 + y),
                    device_id_type=MESH,
                ).start()

            if n == BLOCKS - 1:
                pl.when(i != 4)(send)
            else:
                send()
        return 0

    lax.fori_loop(0, GROUPS, give, 0, unroll=False)

    await_bytes(outgoing.at[pl.ds(0, DEVICES - 2)], a2a_ss)

    @pl.when(jnp.logical_not(has_from))
    def _():
        await_bytes(outgoing.at[0], a2a_ss)

    @pl.when(has_to)
    def _():
        await_bytes(recv.at[OWN, pl.ds(0, 2)], rl_ss.at[OWN])

    @pl.when(has_from)
    def _():
        await_bytes(recv.at[OWN, pl.ds(0, 2)], rl_ss.at[NEAR])

    await_bytes(recv.at[OWN], sib_ss)
    own_back.wait()
    part = back.at[pl.ds(0, DEVICES - 1)]
    await_bytes(part, back_ss)
    await_bytes(part, back_rs)

    slot_iota = lax.broadcasted_iota(jnp.int32, (SLOT, ROWS), 0)
    best = jnp.full((SLOT, ROWS), LOW, jnp.float32)
    for which in range(3):
        turned[...] = back[:, which, 0, :].T
        rest = turned[pl.ds((lax.rem(bme, 8) * 2 + core) * SLOT, SLOT), :]
        parts = []
        for _ in range(3):
            parts.append(rest.astype(jnp.bfloat16))
            rest = rest - parts[-1].astype(jnp.float32)
        slots = jnp.zeros((SLOT, ROWS), jnp.float32)
        for part in parts:
            slots = slots + jnp.dot(part, picks[which], preferred_element_type=jnp.float32)
        if which == NEAR:
            slots = jnp.where(t_ok, slots, LOW)
        best = jnp.maximum(best, slots)
    out[...] = jnp.sum(jnp.where(slot_iota == slot_of, best, 0.0), axis=0, keepdims=True)


def body(embeddings, target, cluster_labels):
    bf, f32, i32 = jnp.bfloat16, jnp.float32, jnp.int32
    dma = pltpu.SemaphoreType.DMA
    result = pl.pallas_call(
        kernel,
        out_shape=jax.ShapeDtypeStruct((1, ROWS), f32),
        in_specs=[pl.BlockSpec(memory_space=pl.ANY)] * 3,
        out_specs=pl.BlockSpec(memory_space=pltpu.VMEM),
        scratch_shapes=[
            pltpu.VMEM((ROWS, E), bf),
            pltpu.VMEM((ROWS, E), bf),
            pltpu.VMEM((DEVICES, SLOT, E), bf),
            pltpu.VMEM((3, 4, 4, 4, 2, SLOT, E), bf),
            pltpu.VMEM((3, ROWS, E), bf),
            pltpu.VMEM((1, ROWS), i32),
            pltpu.VMEM((4, 1, ROWS), i32),
            pltpu.VMEM((4, 1, ROWS), f32),
            pltpu.VMEM((4, 1, ROWS), f32),
            pltpu.VMEM((3, CHUNKS, 1, LANES), f32),
            pltpu.VMEM((3, CHUNKS, 1, LANES), f32),
            pltpu.VMEM((3, 8, ROWS), f32),
            pltpu.VMEM((3, CHUNKS, 1, LANES), f32),
            pltpu.VMEM((3, CHUNKS, 1, LANES), f32),
            pltpu.VMEM((DEVICES, 3, 1, LANES), f32),
            pltpu.VMEM((3, DEVICES, ROWS), bf),
            pltpu.VMEM((LANES, DEVICES), f32),
            dma((4,)),
            dma((4,)),
            dma,
            dma,
            dma, dma,
            dma, dma((2, GROUPS)),
            dma((2,)), dma((2, GROUPS)),
            dma, dma((STAGES,)),
            dma, dma,
            pltpu.SemaphoreType.REGULAR,
        ],
        compiler_params=pltpu.CompilerParams(
            collective_id=0, has_side_effects=True, vmem_limit_bytes=60 * 2**20
        ),
        name="dedup_scores",
    )(embeddings, target.reshape(1, ROWS), cluster_labels.reshape(BLOCKS, 1, ROWS))
    return result.reshape(ROWS)


def solution(mesh):
    return jax.shard_map(
        body,
        mesh=mesh,
        in_specs=(P(("group", "block"), None), P(("group", "block")), P("group")),
        out_specs=P(("group", "block")),
        check_vma=False,
    )
```

```python
import jax
import jax.numpy as jnp
from jax import lax
from jax.experimental import pallas as pl
from jax.experimental.pallas import tpu as pltpu
from jax.sharding import PartitionSpec as P

MESH = pl.DeviceIdType.MESH
E = 1024
ROWS = 1024
GROUPS = 8
BLOCKS = 16
DEVICES = GROUPS * BLOCKS
SLOT = ROWS // DEVICES
LANES = 128
CHUNKS = ROWS // LANES
STAGES = 4
PIECE = ROWS // STAGES
LOW = -2.0
OWN, NEAR, SIB = 0, 1, 2
OFFSETS = (2, 1, 3, 0)


def place_of(block):
    z, y = block // 4, block % 4
    turn = z % 2
    return turn * 4 + y + turn * (3 - 2 * y)


def block_at(half, place):
    turn, r = place // 4, place % 4
    return (2 * half + turn) * 4 + r + turn * (3 - 2 * r)


def partner(block, core):
    place = place_of(block) - 1 + 2 * core
    ok = (place >= 0) & (place < 8)
    return block_at(block // 8, jnp.clip(place, 0, 7)), ok


def kernel(
    emb, tgt_hbm, lab, out,
    raw, unit, outgoing, recv, blk, tgt, lab_loc, lab_out, lab_in, lane_lab, col_lab, col_best, row_best, score, back, picks, turned,
    raw_sem, lab_sem, tgt_sem, self_sem, lab_ss, lab_rs, a2a_ss, a2a_rs, rl_ss, rl_rs, sib_ss, sib_rs,
    back_ss, back_rs, row_sem,
):
    gme = lax.axis_index("group")
    bme = lax.axis_index("block")
    me = gme * BLOCKS + bme
    core = gme % 2
    gsib = gme + 1 - 2 * core
    xme, zme, yme = gme // 2, bme // 4, bme % 4
    place = place_of(bme)
    sum_me = xme + zme + yme
    half = bme // 8
    to_block, has_to = partner(bme, core)
    from_block, has_from = partner(bme, 1 - core)
    dev_sib = (gsib, bme)
    sum_from = xme + from_block // 4 + from_block % 4
    class_me = lax.rem(sum_me, 4)

    raw_copies = []
    for i in range(4):
        rows = pl.ds(i * 256, 256)
        raw_copies.append(pltpu.make_async_copy(emb.at[rows], raw.at[rows], raw_sem.at[i]))
    tgt_copy = pltpu.make_async_copy(tgt_hbm, tgt, tgt_sem)
    lab_copies = []
    for i in range(4):
        b = jnp.clip(2 * place - 1 + i, 0, BLOCKS - 1)
        lab_copies.append(pltpu.make_async_copy(lab.at[b], lab_loc.at[i], lab_sem.at[i]))
    for copy in raw_copies + [tgt_copy] + lab_copies:
        copy.start()

    barrier = pltpu.get_barrier_semaphore()

    row = [lax.rem(bme + i, BLOCKS) for i in range(1, BLOCKS)]
    column = [lax.rem(gme + i, GROUPS) for i in range(1, GROUPS)]
    for block in row:
        pl.semaphore_signal(barrier, inc=1, device_id=(gme, block), device_id_type=MESH)
    for group in column:
        pl.semaphore_signal(barrier, inc=1, device_id=(group, bme), device_id_type=MESH)

    for which in range(3):
        col_best[which] = jnp.full((8, ROWS), LOW, jnp.float32)
        for t in range(CHUNKS):
            row_best[which, t] = jnp.full((1, LANES), LOW, jnp.float32)
            col_lab[which, t] = jnp.full((1, LANES), -1.0, jnp.float32)

    for i in range(4):
        raw_copies[i].wait()
        for j in range(2):
            rows = pl.ds(i * 256 + j * 128, 128)
            values = raw[rows, :].astype(jnp.float32)
            squares = jnp.sum(values * values, axis=1, keepdims=True)
            unit[rows, :] = (values * lax.rsqrt(squares + 1e-06)).astype(jnp.bfloat16)

    tgt_copy.wait()
    target = tgt[...]
    row_block = target // ROWS
    t_core = row_block % 2
    t_group = row_block // (2 * BLOCKS) * 2 + t_core
    t_half = row_block // BLOCKS % 2
    t_place = row_block % BLOCKS // 2
    home = t_group * BLOCKS + block_at(t_half, t_place)
    slot_of = target % SLOT
    t_block = home % BLOCKS
    t_class = (t_group // 2 + t_block // 4 + t_block % 4) % 4
    position = (t_class * 32 + t_block * 2 + t_core) * SLOT + slot_of
    row_iota = lax.broadcasted_iota(jnp.int32, (PIECE, ROWS), 0)

    def permute(q):
        a = lax.rem(class_me + q, 4)
        onehot = jnp.where(row_iota == position - a * PIECE, 1.0, 0.0).astype(jnp.bfloat16)
        picked = jnp.dot(onehot, unit[...], preferred_element_type=jnp.float32)
        slots = PIECE // SLOT
        outgoing[pl.ds(a * slots, slots)] = picked.reshape(slots, SLOT, E).astype(jnp.bfloat16)

    routes = []
    for c in range(2):
        to_core = lax.rem(core + c, 2)
        sign = 2 * to_core - 1
        for dz in OFFSETS:
            for dy in OFFSETS:
                z, y = lax.rem(zme + dz, 4), lax.rem(yme + dy, 4)
                turn = lax.rem(z, 2)
                along = 1 - 2 * turn
                way = sign * along
                on_y = (y + way >= 0) & (y + way <= 3)
                on_z = (y == 3) & (way == 1)
                far_y = {0: way == 0, 1: way == -1, 2: way != 0, 3: way == 1}[dy]
                far_z = {0: turn == 2, 1: turn == 1, 2: turn != 2, 3: turn == 0}[dz]
                second = (on_y & far_y) | (on_z & far_z)
                block = z * 4 + y
                other = jnp.where(on_y, block + way, block + 4 * along)
                routes.append((c, dz, dy, block, jnp.where(second, NEAR, OWN), jnp.where(second, other, block)))

    def send(q, c, x, home_block, which, block):
        to_core = core if c == 0 else 1 - core
        pltpu.make_async_remote_copy(
            outgoing.at[lax.rem(class_me + q, 4) * 32 + home_block * 2 + to_core],
            recv.at[which, class_me, zme, yme, core],
            a2a_ss,
            a2a_rs.at[which, 2 * q + c],
            device_id=(2 * x + to_core, block),
            device_id_type=MESH,
        ).start()

    def send_known(q):
        for c, dz, dy, home_block, which, block in routes:
            dx = (q - dz - dy) % 4
            if dz == 0 and dy == 0:
                if dx or c:
                    send(q, c, lax.rem(xme + dx, 4), home_block, which, block)
            elif c == 0 and dx == 0:

                @pl.when(block != bme)
                def _():
                    send(q, c, xme, home_block, which, block)

    def send_rest(q, _):
        for c, dz, dy, home_block, which, block in routes:
            if dz == 0 and dy == 0:
                continue
            dx = lax.rem(q + 8 - dz - dy, 4)

            def go():
                send(q, c, lax.rem(xme + dx, 4), home_block, which, block)

            if c == 0:
                pl.when(dx != 0)(go)
            else:
                go()
        return 0

    def send_all(q, _):
        permute(q)
        for c, dz, dy, home_block, which, block in routes:
            dx = lax.rem(q + 8 - dz - dy, 4)

            def go():
                send(q, c, lax.rem(xme + dx, 4), home_block, which, block)

            if c == 0 and (dz or dy):
                pl.when((dx != 0) | (block != bme))(go)
            else:
                go()
        return 0

    permute(0)
    pl.semaphore_wait(barrier, len(row) + len(column))
    for block in row:
        pl.semaphore_signal(row_sem, inc=1, device_id=(gme, block), device_id_type=MESH)
    send_known(0)
    pltpu.make_async_copy(
        outgoing.at[class_me * 32 + bme * 2 + core],
        recv.at[OWN, class_me, zme, yme, core],
        a2a_rs.at[OWN, 0],
    ).start()
    permute(1)
    send_known(1)
    pl.semaphore_wait(row_sem, len(row))
    lax.fori_loop(0, 2, send_rest, 0, unroll=False)
    lax.fori_loop(2, STAGES, send_all, 0, unroll=False)

    @pl.when(has_from)
    def _():
        pltpu.make_async_copy(
            outgoing.at[lax.rem(sum_from, 4) * 32 + from_block * 2 + core],
            recv.at[NEAR, class_me, zme, yme, core],
            a2a_rs.at[NEAR, 2 * lax.rem(sum_from - sum_me + 4, 4)],
        ).start()

    for copy in lab_copies:
        copy.wait()
    stored = lax.broadcasted_iota(jnp.int32, (1, ROWS), 1)
    slot_no = stored // SLOT
    s_class, s_block, s_core = slot_no // 32, slot_no % 32 // 2, slot_no % 2
    s_x = (s_class - s_block // 4 - s_block % 4 + 8) % 4
    natural = ((2 * s_x + s_core) * BLOCKS + s_block) * SLOT + stored % SLOT
    lab_all = jnp.concatenate([lab_loc[i] for i in range(4)], axis=0)
    high = lab_all // 256
    halves = jnp.concatenate([high, lab_all - 256 * high], axis=0).astype(jnp.float32).astype(jnp.bfloat16)
    moved = jnp.zeros((8, ROWS), jnp.float32)
    for t in range(CHUNKS):
        move = jnp.where(row_iota[:LANES] == natural - t * LANES, 1.0, 0.0).astype(jnp.bfloat16)
        moved = moved + jnp.dot(
            halves[:, t * LANES : (t + 1) * LANES], move, preferred_element_type=jnp.float32
        )
    lab_new = moved[:4] * 256.0 + moved[4:]
    for i in range(4):
        lab_out[i] = lab_new[i : i + 1]

    lab_copy = pltpu.make_async_remote_copy(
        lab_out, lab_in, lab_ss, lab_rs, device_id=dev_sib, device_id_type=MESH
    )
    lab_copy.start()
    t_to, t_ok = partner(home % BLOCKS, t_core)
    dev_iota = lax.broadcasted_iota(jnp.int32, (DEVICES, ROWS), 0)
    devs = (home, t_group * BLOCKS + t_to, home + (1 - 2 * t_core) * BLOCKS)
    for which in range(3):
        picks[which] = jnp.where(dev_iota == devs[which], 1.0, 0.0).astype(jnp.bfloat16)

    lab_copy.wait()
    labels = [
        jnp.where(half == core, lab_out[i], lab_in[i]) for i in range(4)
    ]
    is0 = core == 0
    sides = [
        jnp.where(is0, labels[1], labels[2]),
        jnp.where(has_from, jnp.where(is0, labels[3], labels[0]), -2.0),
        jnp.where(is0, labels[2], labels[1]),
    ]
    for which in range(3):
        for t in range(CHUNKS):
            lane_lab[which, t] = sides[which][:, t * LANES : (t + 1) * LANES]

    eight = recv.at[OWN, 0, 0]
    sixteen = recv.at[OWN, 0, pl.ds(0, 2)]
    thirty_two = recv.at[OWN, 0]

    def await_bytes(ref, sem):
        pltpu.make_async_copy(ref, ref, sem).wait()

    def hand_on(which, n, a, c, dy, dz, block):
        for step in range(2):
            yy = lax.rem(yme + step * dy + 4, 4)
            zz = lax.rem(zme + step * dz + 4, 4)

            def go(src, dst):
                pltpu.make_async_remote_copy(
                    src, dst, rl_ss.at[which], rl_rs.at[1 - which, n], device_id=(gme, block), device_id_type=MESH
                ).start()

            @pl.when(dy != 0)
            def _():
                go(recv.at[which, a, :, yy, c], recv.at[1 - which, a, :, yy, c])

            @pl.when(dy == 0)
            def _():
                go(recv.at[which, a, zz, :, c], recv.at[1 - which, a, zz, :, c])

    def own_class(q):
        return lax.rem(sum_me - q + 4, 4)

    def near_class(q):
        return lax.rem(sum_from - q + 4, 4)

    def first(q, c):
        n = 2 * q + c
        from_core = lax.rem(core + c, 2)

        @pl.when(has_to)
        def _():
            await_bytes(eight, a2a_rs.at[OWN, n])
            hand_on(OWN, n, own_class(q), from_core, yme - to_block % 4, zme - to_block // 4, to_block)

        @pl.when(jnp.logical_not(has_to))
        def _():
            await_bytes(sixteen, a2a_rs.at[OWN, n])

        @pl.when(has_from)
        def _():
            await_bytes(eight, a2a_rs.at[NEAR, n])
            hand_on(NEAR, n, near_class(q), from_core, yme - from_block % 4, zme - from_block // 4, from_block)

    def lay_out(which, x):
        got = recv[which, x].astype(jnp.float32)
        blk[which, pl.ds(x * PIECE, PIECE), :] = got.reshape(PIECE, E).astype(jnp.bfloat16)
        for c in range(2):
            col_lab[which, 2 * x + c] = lane_lab[which, 2 * x + c]

    r_iota = lax.broadcasted_iota(jnp.int32, (PIECE, LANES), 0)
    c_iota = lax.broadcasted_iota(jnp.int32, (PIECE, LANES), 1)
    ahead = r_iota - c_iota

    def product(a, x, b, same_block=False):
        gram = lax.dot_general(
            blk[a, pl.ds(x * PIECE, PIECE), :],
            blk[b],
            (((1,), (1,)), ((), ())),
            preferred_element_type=jnp.float32,
        )
        a_lab = jnp.concatenate(
            [jnp.broadcast_to(lane_lab[a, 2 * x + c], (LANES, LANES)).T for c in range(2)], axis=0
        )
        rows_best = jnp.full((PIECE, LANES), LOW, jnp.float32)
        for t in range(CHUNKS):
            cut = slice(t * LANES, (t + 1) * LANES)
            same = a_lab == col_lab[b, t]
            if same_block:
                same = same & (ahead != t * LANES - x * PIECE)
            masked = jnp.where(same, gram[:, cut], LOW)
            rows_best = jnp.maximum(rows_best, masked)
            col_best[b, :, cut] = jnp.maximum(
                col_best[b, :, cut], jnp.max(masked.reshape(PIECE // 8, 8, LANES), axis=0)
            )
        return rows_best

    def fold_rows(which, x, rows_best):
        for c in range(2):
            line = jnp.max(rows_best[c * LANES : (c + 1) * LANES].T, axis=0, keepdims=True)
            row_best[which, 2 * x + c] = jnp.maximum(row_best[which, 2 * x + c], line)

    def complete(q):
        x, w = own_class(q), near_class(q)

        @pl.when(has_to)
        def _():
            for c in range(2):
                await_bytes(eight, rl_rs.at[OWN, 2 * q + c])

        pltpu.make_async_remote_copy(
            recv.at[OWN, x], recv.at[SIB, x], sib_ss, sib_rs.at[q], device_id=dev_sib, device_id_type=MESH
        ).start()
        lay_out(OWN, x)

        @pl.when(has_from)
        def _():
            for c in range(2):
                await_bytes(eight, rl_rs.at[NEAR, 2 * q + c])
            lay_out(NEAR, w)

        own_rows = product(OWN, x, OWN, same_block=True)
        fold_rows(OWN, x, jnp.maximum(own_rows, product(OWN, x, NEAR)))
        fold_rows(NEAR, w, product(NEAR, w, OWN))

    third = 1 - core

    def sibling(q):
        x, w = own_class(q), near_class(q)
        await_bytes(thirty_two, sib_rs.at[q])
        lay_out(SIB, x)
        fold_rows(SIB, x, product(SIB, x, third))
        v = jnp.where(core == 0, w, x)
        fold_rows(third, v, product(third, v, SIB))

    def step(s, _):
        @pl.when(s < STAGES)
        def _():
            first(s, 0)
            first(s, 1)

        @pl.when(s >= 2)
        def _():
            sibling(s - 2)

        @pl.when((s >= 1) & (s < STAGES + 1))
        def _():
            complete(s - 1)

        return 0

    lax.fori_loop(0, STAGES + 2, step, 0, unroll=False)

    lines = []
    for which in range(3):
        cols = [
            jnp.max(col_best[which, :, t * LANES : (t + 1) * LANES], axis=0, keepdims=True)
            for t in range(CHUNKS)
        ]
        lines.append(jnp.maximum(jnp.concatenate(cols, axis=0), row_best[which][:, 0, :]))
    lane = lax.broadcasted_iota(jnp.int32, (CHUNKS, LANES), 1)
    for j in range(LANES // 16):
        own, near, sib = (
            pltpu.roll(line, (16 * which - 16 * j) % LANES, 1) for which, line in enumerate(lines)
        )
        packed = jnp.where(lane < 16, own, jnp.where(lane < 32, near, sib))
        for t in range(CHUNKS):
            score[j, t] = packed[t : t + 1]

    own_back = pltpu.make_async_copy(
        score.at[lax.rem(bme, 8), 2 * class_me + zme // 2], back.at[me], self_sem
    )
    own_back.start()

    near_coords = [(lax.rem(zme + dz, 4), lax.rem(yme + dy, 4)) for dz in OFFSETS for dy in OFFSETS]

    def give(i, _):
        group = lax.rem(gme + 4 + i, GROUPS)
        for n, (z, y) in enumerate(near_coords):
            chunk = 2 * lax.rem(group // 2 + z + y, 4) + z // 2

            def send():
                pltpu.make_async_remote_copy(
                    score.at[lax.rem(z, 2) * 4 + y, chunk],
                    back.at[me],
                    back_ss,
                    back_rs,
                    device_id=(group, z * 4 + y),
                    device_id_type=MESH,
                ).start()

            if n == BLOCKS - 1:
                pl.when(i != 4)(send)
            else:
                send()
        return 0

    lax.fori_loop(0, GROUPS, give, 0, unroll=False)

    await_bytes(outgoing.at[pl.ds(0, DEVICES - 2)], a2a_ss)

    @pl.when(jnp.logical_not(has_from))
    def _():
        await_bytes(outgoing.at[0], a2a_ss)

    @pl.when(has_to)
    def _():
        await_bytes(recv.at[OWN, pl.ds(0, 2)], rl_ss.at[OWN])

    @pl.when(has_from)
    def _():
        await_bytes(recv.at[OWN, pl.ds(0, 2)], rl_ss.at[NEAR])

    await_bytes(recv.at[OWN], sib_ss)
    own_back.wait()
    part = back.at[pl.ds(0, DEVICES - 1)]
    await_bytes(part, back_ss)
    await_bytes(part, back_rs)

    slot_iota = lax.broadcasted_iota(jnp.int32, (SLOT, ROWS), 0)
    best = jnp.full((SLOT, ROWS), LOW, jnp.float32)
    turned[...] = back[:, 0, :].T
    for which in range(3):
        rest = turned[pl.ds(16 * which + core * SLOT, SLOT), :]
        parts = []
        for _ in range(3):
            parts.append(rest.astype(jnp.bfloat16))
            rest = rest - parts[-1].astype(jnp.float32)
        slots = jnp.zeros((SLOT, ROWS), jnp.float32)
        for part in parts:
            slots = slots + jnp.dot(part, picks[which], preferred_element_type=jnp.float32)
        if which == NEAR:
            slots = jnp.where(t_ok, slots, LOW)
        best = jnp.maximum(best, slots)
    out[...] = jnp.sum(jnp.where(slot_iota == slot_of, best, 0.0), axis=0, keepdims=True)


def body(embeddings, target, cluster_labels):
    bf, f32, i32 = jnp.bfloat16, jnp.float32, jnp.int32
    dma = pltpu.SemaphoreType.DMA
    result = pl.pallas_call(
        kernel,
        out_shape=jax.ShapeDtypeStruct((1, ROWS), f32),
        in_specs=[pl.BlockSpec(memory_space=pl.ANY)] * 3,
        out_specs=pl.BlockSpec(memory_space=pltpu.VMEM),
        scratch_shapes=[
            pltpu.VMEM((ROWS, E), bf),
            pltpu.VMEM((ROWS, E), bf),
            pltpu.VMEM((DEVICES, SLOT, E), bf),
            pltpu.VMEM((3, 4, 4, 4, 2, SLOT, E), bf),
            pltpu.VMEM((3, ROWS, E), bf),
            pltpu.VMEM((1, ROWS), i32),
            pltpu.VMEM((4, 1, ROWS), i32),
            pltpu.VMEM((4, 1, ROWS), f32),
            pltpu.VMEM((4, 1, ROWS), f32),
            pltpu.VMEM((3, CHUNKS, 1, LANES), f32),
            pltpu.VMEM((3, CHUNKS, 1, LANES), f32),
            pltpu.VMEM((3, 8, ROWS), f32),
            pltpu.VMEM((3, CHUNKS, 1, LANES), f32),
            pltpu.VMEM((LANES // 16, CHUNKS, 1, LANES), f32),
            pltpu.VMEM((DEVICES, 1, LANES), f32),
            pltpu.VMEM((3, DEVICES, ROWS), bf),
            pltpu.VMEM((LANES, DEVICES), f32),
            dma((4,)),
            dma((4,)),
            dma,
            dma,
            dma, dma,
            dma, dma((2, GROUPS)),
            dma((2,)), dma((2, GROUPS)),
            dma, dma((STAGES,)),
            dma, dma,
            pltpu.SemaphoreType.REGULAR,
        ],
        compiler_params=pltpu.CompilerParams(
            collective_id=0, has_side_effects=True, vmem_limit_bytes=60 * 2**20
        ),
        name="dedup_scores",
    )(embeddings, target.reshape(1, ROWS), cluster_labels.reshape(BLOCKS, 1, ROWS))
    return result.reshape(ROWS)


def solution(mesh):
    return jax.shard_map(
        body,
        mesh=mesh,
        in_specs=(P(("group", "block"), None), P(("group", "block")), P("group")),
        out_specs=P(("group", "block")),
        check_vma=False,
    )
```

```python
import jax
import jax.numpy as jnp
from jax import lax
from jax.experimental import pallas as pl
from jax.experimental.pallas import tpu as pltpu
from jax.sharding import PartitionSpec as P

MESH = pl.DeviceIdType.MESH
E = 1024
ROWS = 1024
GROUPS = 8
BLOCKS = 16
DEVICES = GROUPS * BLOCKS
SLOT = ROWS // DEVICES
LANES = 128
CHUNKS = ROWS // LANES
STAGES = 4
PIECE = ROWS // STAGES
LOW = -2.0
OWN, NEAR, SIB = 0, 1, 2
OFFSETS = (2, 1, 3, 0)


def place_of(block):
    z, y = block // 4, block % 4
    turn = z % 2
    return turn * 4 + y + turn * (3 - 2 * y)


def block_at(half, place):
    turn, r = place // 4, place % 4
    return (2 * half + turn) * 4 + r + turn * (3 - 2 * r)


def partner(block, core):
    place = place_of(block) - 1 + 2 * core
    ok = (place >= 0) & (place < 8)
    return block_at(block // 8, jnp.clip(place, 0, 7)), ok


def kernel(
    emb, tgt_hbm, lab, out,
    raw, unit, outgoing, recv, blk, tgt, lab_loc, lab_out, lab_in, lane_lab, col_lab, col_best, row_best, score, back, picks, turned,
    raw_sem, lab_sem, tgt_sem, self_sem, lab_ss, lab_rs, a2a_ss, a2a_rs, rl_ss, rl_rs, sib_ss, sib_rs,
    back_ss, back_rs, plane_sem,
):
    gme = lax.axis_index("group")
    bme = lax.axis_index("block")
    me = gme * BLOCKS + bme
    core = gme % 2
    gsib = gme + 1 - 2 * core
    xme, zme, yme = gme // 2, bme // 4, bme % 4
    place = place_of(bme)
    sum_me = xme + zme + yme
    half = bme // 8
    to_block, has_to = partner(bme, core)
    from_block, has_from = partner(bme, 1 - core)
    dev_sib = (gsib, bme)
    sum_from = xme + from_block // 4 + from_block % 4
    class_me = lax.rem(sum_me, 4)

    raw_copies = []
    for i in range(4):
        rows = pl.ds(i * 256, 256)
        raw_copies.append(pltpu.make_async_copy(emb.at[rows], raw.at[rows], raw_sem.at[i]))
    tgt_copy = pltpu.make_async_copy(tgt_hbm, tgt, tgt_sem)
    lab_copies = []
    for i in range(4):
        b = jnp.clip(2 * place - 1 + i, 0, BLOCKS - 1)
        lab_copies.append(pltpu.make_async_copy(lab.at[b], lab_loc.at[i], lab_sem.at[i]))
    for copy in raw_copies + [tgt_copy] + lab_copies:
        copy.start()

    barrier = pltpu.get_barrier_semaphore()

    images = [2 * lax.rem(xme + dx, 4) + core for dx in (2, 1, 3)]

    def greet(i, _):
        block = lax.rem(bme + i, BLOCKS)
        for group in (gme, gsib):
            pl.semaphore_signal(barrier, inc=1, device_id=(group, block), device_id_type=MESH)
        return 0

    lax.fori_loop(1, BLOCKS, greet, 0, unroll=False)
    for group in images:
        pl.semaphore_signal(barrier, inc=1, device_id=(group, bme), device_id_type=MESH)
    pl.semaphore_signal(barrier, inc=1, device_id=dev_sib, device_id_type=MESH)

    for which in range(3):
        col_best[which] = jnp.full((8, ROWS), LOW, jnp.float32)
        for t in range(CHUNKS):
            row_best[which, t] = jnp.full((1, LANES), LOW, jnp.float32)
            col_lab[which, t] = jnp.full((1, LANES), -1.0, jnp.float32)

    for i in range(4):
        raw_copies[i].wait()
        for j in range(2):
            rows = pl.ds(i * 256 + j * 128, 128)
            values = raw[rows, :].astype(jnp.float32)
            squares = jnp.sum(values * values, axis=1, keepdims=True)
            unit[rows, :] = (values * lax.rsqrt(squares + 1e-06)).astype(jnp.bfloat16)

    tgt_copy.wait()
    target = tgt[...]
    row_block = target // ROWS
    t_core = row_block % 2
    t_group = row_block // (2 * BLOCKS) * 2 + t_core
    t_half = row_block // BLOCKS % 2
    t_place = row_block % BLOCKS // 2
    home = t_group * BLOCKS + block_at(t_half, t_place)
    slot_of = target % SLOT
    t_block = home % BLOCKS
    t_class = (t_group // 2 + t_block // 4 + t_block % 4) % 4
    position = (t_class * 32 + t_block * 2 + t_core) * SLOT + slot_of
    row_iota = lax.broadcasted_iota(jnp.int32, (PIECE, ROWS), 0)

    def permute(q):
        a = lax.rem(class_me + q, 4)
        onehot = jnp.where(row_iota == position - a * PIECE, 1.0, 0.0).astype(jnp.bfloat16)
        picked = jnp.dot(onehot, unit[...], preferred_element_type=jnp.float32)
        slots = PIECE // SLOT
        outgoing[pl.ds(a * slots, slots)] = picked.reshape(slots, SLOT, E).astype(jnp.bfloat16)

    routes = []
    for c in range(2):
        to_core = lax.rem(core + c, 2)
        sign = 2 * to_core - 1
        for dz in OFFSETS:
            for dy in OFFSETS:
                z, y = lax.rem(zme + dz, 4), lax.rem(yme + dy, 4)
                turn = lax.rem(z, 2)
                along = 1 - 2 * turn
                way = sign * along
                on_y = (y + way >= 0) & (y + way <= 3)
                on_z = (y == 3) & (way == 1)
                far_y = {0: way == 0, 1: way == -1, 2: way != 0, 3: way == 1}[dy]
                far_z = {0: turn == 2, 1: turn == 1, 2: turn != 2, 3: turn == 0}[dz]
                second = (on_y & far_y) | (on_z & far_z)
                block = z * 4 + y
                other = jnp.where(on_y, block + way, block + 4 * along)
                target = jnp.where(second, other, block)
                hop = (on_y & (lax.rem(target, 4) != yme)) | (on_z & (target // 4 != zme))
                which = jnp.where(second, NEAR, OWN)
                routes.append((c, dz, dy, block, (which, jnp.where(hop, 1, 0)), target))

    def send(q, c, x, home_block, which, block):
        to_core = core if c == 0 else 1 - core
        pltpu.make_async_remote_copy(
            outgoing.at[lax.rem(class_me + q, 4) * 32 + home_block * 2 + to_core],
            recv.at[which[0], class_me, zme, yme, core],
            a2a_ss,
            a2a_rs.at[which[0], 2 * q + c, which[1]],
            device_id=(2 * x + to_core, block),
            device_id_type=MESH,
        ).start()

    def send_known(q):
        for c, dz, dy, home_block, which, block in routes:
            if (dz + dy) % 4 != q:
                continue

            def go():
                send(q, c, xme, home_block, which, block)

            if c == 0:
                pl.when(block != bme)(go)
            else:
                go()

    def send_rest(q, dxs):
        for c, dz, dy, home_block, which, block in routes:
            dx = (q - dz - dy) % 4
            if dx:
                send(q, c, lax.rem(xme + dx, 4), home_block, which, block)

    def here(dx):
        pl.semaphore_wait(plane_sem.at[dx - 1], 1)

    permute(0)
    pl.semaphore_wait(barrier, 2 * BLOCKS - 1 + len(images))
    for dx, group in zip((2, 1, 3), images):
        pl.semaphore_signal(plane_sem.at[3 - dx], inc=1, device_id=(group, bme), device_id_type=MESH)
    for q in range(2):
        if q:
            permute(q)
        send_known(q)
    pltpu.make_async_copy(
        outgoing.at[class_me * 32 + bme * 2 + core],
        recv.at[OWN, class_me, zme, yme, core],
        a2a_rs.at[OWN, 0, 0],
    ).start()

    for dx in (1, 3, 2):
        here(dx)
    send_rest(0, ())
    send_rest(1, ())
    for q in range(2, STAGES):
        permute(q)
        send_known(q)
    send_rest(2, ())
    send_rest(3, ())

    @pl.when(has_from)
    def _():
        pltpu.make_async_copy(
            outgoing.at[lax.rem(sum_from, 4) * 32 + from_block * 2 + core],
            recv.at[NEAR, class_me, zme, yme, core],
            a2a_rs.at[NEAR, 2 * lax.rem(sum_from - sum_me + 4, 4), 0],
        ).start()

    for copy in lab_copies:
        copy.wait()
    stored = lax.broadcasted_iota(jnp.int32, (1, ROWS), 1)
    slot_no = stored // SLOT
    s_class, s_block, s_core = slot_no // 32, slot_no % 32 // 2, slot_no % 2
    s_x = (s_class - s_block // 4 - s_block % 4 + 8) % 4
    natural = ((2 * s_x + s_core) * BLOCKS + s_block) * SLOT + stored % SLOT
    lab_all = jnp.concatenate([lab_loc[i] for i in range(4)], axis=0)
    high = lab_all // 256
    halves = jnp.concatenate([high, lab_all - 256 * high], axis=0).astype(jnp.float32).astype(jnp.bfloat16)
    moved = jnp.zeros((8, ROWS), jnp.float32)
    for t in range(CHUNKS):
        move = jnp.where(row_iota[:LANES] == natural - t * LANES, 1.0, 0.0).astype(jnp.bfloat16)
        moved = moved + jnp.dot(
            halves[:, t * LANES : (t + 1) * LANES], move, preferred_element_type=jnp.float32
        )
    lab_new = moved[:4] * 256.0 + moved[4:]
    for i in range(4):
        lab_out[i] = lab_new[i : i + 1]

    lab_copy = pltpu.make_async_remote_copy(
        lab_out, lab_in, lab_ss, lab_rs, device_id=dev_sib, device_id_type=MESH
    )
    lab_copy.start()
    t_to, t_ok = partner(home % BLOCKS, t_core)
    dev_iota = lax.broadcasted_iota(jnp.int32, (DEVICES, ROWS), 0)
    devs = (home, t_group * BLOCKS + t_to, home + (1 - 2 * t_core) * BLOCKS)
    for which in range(3):
        picks[which] = jnp.where(dev_iota == devs[which], 1.0, 0.0).astype(jnp.bfloat16)

    lab_copy.wait()
    labels = [
        jnp.where(half == core, lab_out[i], lab_in[i]) for i in range(4)
    ]
    is0 = core == 0
    sides = [
        jnp.where(is0, labels[1], labels[2]),
        jnp.where(has_from, jnp.where(is0, labels[3], labels[0]), -2.0),
        jnp.where(is0, labels[2], labels[1]),
    ]
    for which in range(3):
        for t in range(CHUNKS):
            lane_lab[which, t] = sides[which][:, t * LANES : (t + 1) * LANES]

    four = recv.at[OWN, 0, 0, pl.ds(0, 2)]
    eight = recv.at[OWN, 0, 0]
    sixteen = recv.at[OWN, 0, pl.ds(0, 2)]
    thirty_two = recv.at[OWN, 0]

    def await_bytes(ref, sem):
        pltpu.make_async_copy(ref, ref, sem).wait()

    def hand_on(which, n, a, c, dy, dz, block, steps):
        for step in steps:
            await_bytes(four, a2a_rs.at[which, n, step])
            yy = lax.rem(yme + step * dy + 4, 4)
            zz = lax.rem(zme + step * dz + 4, 4)

            def go(src, dst):
                pltpu.make_async_remote_copy(
                    src, dst, rl_ss.at[which], rl_rs.at[1 - which, n], device_id=(gme, block), device_id_type=MESH
                ).start()

            @pl.when(dy != 0)
            def _():
                go(recv.at[which, a, :, yy, c], recv.at[1 - which, a, :, yy, c])

            @pl.when(dy == 0)
            def _():
                go(recv.at[which, a, zz, :, c], recv.at[1 - which, a, zz, :, c])

    def own_class(q):
        return lax.rem(sum_me - q + 4, 4)

    def near_class(q):
        return lax.rem(sum_from - q + 4, 4)

    def first(q, c):
        n = 2 * q + c
        from_core = lax.rem(core + c, 2)

        for step in range(2):

            @pl.when(has_to)
            def _():
                hand_on(OWN, n, own_class(q), from_core, yme - to_block % 4, zme - to_block // 4, to_block, (step,))

            @pl.when(has_from)
            def _():
                hand_on(
                    NEAR, n, near_class(q), from_core, yme - from_block % 4, zme - from_block // 4, from_block, (step,)
                )

        @pl.when(jnp.logical_not(has_to))
        def _():
            await_bytes(sixteen, a2a_rs.at[OWN, n, 0])

    def lay_out(which, x):
        got = recv[which, x].astype(jnp.float32)
        blk[which, pl.ds(x * PIECE, PIECE), :] = got.reshape(PIECE, E).astype(jnp.bfloat16)
        for c in range(2):
            col_lab[which, 2 * x + c] = lane_lab[which, 2 * x + c]

    r_iota = lax.broadcasted_iota(jnp.int32, (PIECE, LANES), 0)
    c_iota = lax.broadcasted_iota(jnp.int32, (PIECE, LANES), 1)
    ahead = r_iota - c_iota

    def product(a, x, b, same_block=False):
        gram = lax.dot_general(
            blk[a, pl.ds(x * PIECE, PIECE), :],
            blk[b],
            (((1,), (1,)), ((), ())),
            preferred_element_type=jnp.float32,
        )
        a_lab = jnp.concatenate(
            [jnp.broadcast_to(lane_lab[a, 2 * x + c], (LANES, LANES)).T for c in range(2)], axis=0
        )
        rows_best = jnp.full((PIECE, LANES), LOW, jnp.float32)
        for t in range(CHUNKS):
            cut = slice(t * LANES, (t + 1) * LANES)
            same = a_lab == col_lab[b, t]
            if same_block:
                same = same & (ahead != t * LANES - x * PIECE)
            masked = jnp.where(same, gram[:, cut], LOW)
            rows_best = jnp.maximum(rows_best, masked)
            col_best[b, :, cut] = jnp.maximum(
                col_best[b, :, cut], jnp.max(masked.reshape(PIECE // 8, 8, LANES), axis=0)
            )
        return rows_best

    def fold_rows(which, x, rows_best):
        for c in range(2):
            line = jnp.max(rows_best[c * LANES : (c + 1) * LANES].T, axis=0, keepdims=True)
            row_best[which, 2 * x + c] = jnp.maximum(row_best[which, 2 * x + c], line)

    def complete(q):
        x, w = own_class(q), near_class(q)

        @pl.when(has_to)
        def _():
            for c in range(2):
                await_bytes(eight, rl_rs.at[OWN, 2 * q + c])

        pltpu.make_async_remote_copy(
            recv.at[OWN, x], recv.at[SIB, x], sib_ss, sib_rs.at[q], device_id=dev_sib, device_id_type=MESH
        ).start()
        lay_out(OWN, x)

        @pl.when(has_from)
        def _():
            for c in range(2):
                await_bytes(eight, rl_rs.at[NEAR, 2 * q + c])
            lay_out(NEAR, w)

        own_rows = product(OWN, x, OWN, same_block=True)
        fold_rows(OWN, x, jnp.maximum(own_rows, product(OWN, x, NEAR)))
        fold_rows(NEAR, w, product(NEAR, w, OWN))

    third = 1 - core

    def sibling(q):
        x, w = own_class(q), near_class(q)
        await_bytes(thirty_two, sib_rs.at[q])
        lay_out(SIB, x)
        fold_rows(SIB, x, product(SIB, x, third))
        v = jnp.where(core == 0, w, x)
        fold_rows(third, v, product(third, v, SIB))

    def step(s, _):
        @pl.when(s < STAGES)
        def _():
            first(s, 0)
            first(s, 1)

        @pl.when(s >= 2)
        def _():
            sibling(s - 2)

        @pl.when((s >= 1) & (s < STAGES + 1))
        def _():
            complete(s - 1)

        return 0

    lax.fori_loop(0, STAGES + 2, step, 0, unroll=False)

    lines = []
    for which in range(3):
        cols = [
            jnp.max(col_best[which, :, t * LANES : (t + 1) * LANES], axis=0, keepdims=True)
            for t in range(CHUNKS)
        ]
        lines.append(jnp.maximum(jnp.concatenate(cols, axis=0), row_best[which][:, 0, :]))
    lane = lax.broadcasted_iota(jnp.int32, (CHUNKS, LANES), 1)
    for j in range(LANES // 16):
        own, near, sib = (
            pltpu.roll(line, (16 * which - 16 * j) % LANES, 1) for which, line in enumerate(lines)
        )
        packed = jnp.where(lane < 16, own, jnp.where(lane < 32, near, sib))
        for t in range(CHUNKS):
            score[j, t] = packed[t : t + 1]

    own_back = pltpu.make_async_copy(
        score.at[lax.rem(bme, 8), 2 * class_me + zme // 2], back.at[me], self_sem
    )
    own_back.start()

    near_coords = [(lax.rem(zme + dz, 4), lax.rem(yme + dy, 4)) for dz in OFFSETS for dy in OFFSETS]

    def give(i, _):
        group = lax.rem(gme + 4 + i, GROUPS)
        for n, (z, y) in enumerate(near_coords):
            chunk = 2 * lax.rem(group // 2 + z + y, 4) + z // 2

            def send():
                pltpu.make_async_remote_copy(
                    score.at[lax.rem(z, 2) * 4 + y, chunk],
                    back.at[me],
                    back_ss,
                    back_rs,
                    device_id=(group, z * 4 + y),
                    device_id_type=MESH,
                ).start()

            if n == BLOCKS - 1:
                pl.when(i != 4)(send)
            else:
                send()
        return 0

    lax.fori_loop(0, GROUPS, give, 0, unroll=False)

    await_bytes(outgoing.at[pl.ds(0, DEVICES - 2)], a2a_ss)

    @pl.when(jnp.logical_not(has_from))
    def _():
        await_bytes(outgoing.at[0], a2a_ss)

    @pl.when(has_to)
    def _():
        await_bytes(recv.at[OWN, pl.ds(0, 2)], rl_ss.at[OWN])

    @pl.when(has_from)
    def _():
        await_bytes(recv.at[OWN, pl.ds(0, 2)], rl_ss.at[NEAR])

    await_bytes(recv.at[OWN], sib_ss)
    own_back.wait()
    part = back.at[pl.ds(0, DEVICES - 1)]
    await_bytes(part, back_ss)
    await_bytes(part, back_rs)

    slot_iota = lax.broadcasted_iota(jnp.int32, (SLOT, ROWS), 0)
    best = jnp.full((SLOT, ROWS), LOW, jnp.float32)
    turned[...] = back[:, 0, :].T
    for which in range(3):
        rest = turned[pl.ds(16 * which + core * SLOT, SLOT), :]
        parts = []
        for _ in range(3):
            parts.append(rest.astype(jnp.bfloat16))
            rest = rest - parts[-1].astype(jnp.float32)
        slots = jnp.zeros((SLOT, ROWS), jnp.float32)
        for part in parts:
            slots = slots + jnp.dot(part, picks[which], preferred_element_type=jnp.float32)
        if which == NEAR:
            slots = jnp.where(t_ok, slots, LOW)
        best = jnp.maximum(best, slots)
    out[...] = jnp.sum(jnp.where(slot_iota == slot_of, best, 0.0), axis=0, keepdims=True)


def body(embeddings, target, cluster_labels):
    bf, f32, i32 = jnp.bfloat16, jnp.float32, jnp.int32
    dma = pltpu.SemaphoreType.DMA
    result = pl.pallas_call(
        kernel,
        out_shape=jax.ShapeDtypeStruct((1, ROWS), f32),
        in_specs=[pl.BlockSpec(memory_space=pl.ANY)] * 3,
        out_specs=pl.BlockSpec(memory_space=pltpu.VMEM),
        scratch_shapes=[
            pltpu.VMEM((ROWS, E), bf),
            pltpu.VMEM((ROWS, E), bf),
            pltpu.VMEM((DEVICES, SLOT, E), bf),
            pltpu.VMEM((3, 4, 4, 4, 2, SLOT, E), bf),
            pltpu.VMEM((3, ROWS, E), bf),
            pltpu.VMEM((1, ROWS), i32),
            pltpu.VMEM((4, 1, ROWS), i32),
            pltpu.VMEM((4, 1, ROWS), f32),
            pltpu.VMEM((4, 1, ROWS), f32),
            pltpu.VMEM((3, CHUNKS, 1, LANES), f32),
            pltpu.VMEM((3, CHUNKS, 1, LANES), f32),
            pltpu.VMEM((3, 8, ROWS), f32),
            pltpu.VMEM((3, CHUNKS, 1, LANES), f32),
            pltpu.VMEM((LANES // 16, CHUNKS, 1, LANES), f32),
            pltpu.VMEM((DEVICES, 1, LANES), f32),
            pltpu.VMEM((3, DEVICES, ROWS), bf),
            pltpu.VMEM((LANES, DEVICES), f32),
            dma((4,)),
            dma((4,)),
            dma,
            dma,
            dma, dma,
            dma, dma((2, GROUPS, 2)),
            dma((2,)), dma((2, GROUPS)),
            dma, dma((STAGES,)),
            dma, dma,
            pltpu.SemaphoreType.REGULAR((3,)),
        ],
        compiler_params=pltpu.CompilerParams(
            collective_id=0, has_side_effects=True, vmem_limit_bytes=60 * 2**20
        ),
        name="dedup_scores",
    )(embeddings, target.reshape(1, ROWS), cluster_labels.reshape(BLOCKS, 1, ROWS))
    return result.reshape(ROWS)


def solution(mesh):
    return jax.shard_map(
        body,
        mesh=mesh,
        in_specs=(P(("group", "block"), None), P(("group", "block")), P("group")),
        out_specs=P(("group", "block")),
        check_vma=False,
    )
```

```python
import jax
import jax.numpy as jnp
from jax import lax
from jax.experimental import pallas as pl
from jax.experimental.pallas import tpu as pltpu
from jax.sharding import PartitionSpec as P

MESH = pl.DeviceIdType.MESH
E = 1024
ROWS = 1024
GROUPS = 8
BLOCKS = 16
DEVICES = GROUPS * BLOCKS
SLOT = ROWS // DEVICES
LANES = 128
CHUNKS = ROWS // LANES
STAGES = 4
PIECE = ROWS // STAGES
LOW = -2.0
OWN, NEAR, SIB = 0, 1, 2
OFFSETS = (2, 1, 3, 0)


def place_of(block):
    z, y = block // 4, block % 4
    turn = z % 2
    return turn * 4 + y + turn * (3 - 2 * y)


def block_at(half, place):
    turn, r = place // 4, place % 4
    return (2 * half + turn) * 4 + r + turn * (3 - 2 * r)


def partner(block, core):
    place = place_of(block) - 1 + 2 * core
    ok = (place >= 0) & (place < 8)
    return block_at(block // 8, jnp.clip(place, 0, 7)), ok


def kernel(
    emb, tgt_hbm, lab, out,
    raw, unit, outgoing, recv, blk, tgt, lab_loc, lab_out, lab_in, lane_lab, col_lab, col_best, row_best, score, back, picks, turned,
    raw_sem, lab_sem, tgt_sem, self_sem, lab_ss, lab_rs, a2a_ss, a2a_rs, rl_ss, rl_rs, sib_ss, sib_rs,
    back_ss, back_rs, plane_sem,
):
    gme = lax.axis_index("group")
    bme = lax.axis_index("block")
    me = gme * BLOCKS + bme
    core = gme % 2
    gsib = gme + 1 - 2 * core
    xme, zme, yme = gme // 2, bme // 4, bme % 4
    place = place_of(bme)
    sum_me = xme + zme + yme
    half = bme // 8
    to_block, has_to = partner(bme, core)
    from_block, has_from = partner(bme, 1 - core)
    dev_sib = (gsib, bme)
    sum_from = xme + from_block // 4 + from_block % 4
    class_me = lax.rem(sum_me, 4)

    raw_copies = []
    for i in range(4):
        rows = pl.ds(i * 256, 256)
        raw_copies.append(pltpu.make_async_copy(emb.at[rows], raw.at[rows], raw_sem.at[i]))
    tgt_copy = pltpu.make_async_copy(tgt_hbm, tgt, tgt_sem)
    lab_copies = []
    for i in range(4):
        b = jnp.clip(2 * place - 1 + i, 0, BLOCKS - 1)
        lab_copies.append(pltpu.make_async_copy(lab.at[b], lab_loc.at[i], lab_sem.at[i]))
    for copy in raw_copies + [tgt_copy] + lab_copies:
        copy.start()

    barrier = pltpu.get_barrier_semaphore()

    images = [2 * lax.rem(xme + dx, 4) + core for dx in (2, 1, 3)]

    def greet(i, _):
        block = lax.rem(bme + i, BLOCKS)
        for group in (gme, gsib):
            pl.semaphore_signal(barrier, inc=1, device_id=(group, block), device_id_type=MESH)
        return 0

    lax.fori_loop(1, BLOCKS, greet, 0, unroll=False)
    for group in images:
        pl.semaphore_signal(barrier, inc=1, device_id=(group, bme), device_id_type=MESH)
    pl.semaphore_signal(barrier, inc=1, device_id=dev_sib, device_id_type=MESH)

    for which in range(3):
        col_best[which] = jnp.full((8, ROWS), LOW, jnp.float32)
        for t in range(CHUNKS):
            row_best[which, t] = jnp.full((1, LANES), LOW, jnp.float32)
            col_lab[which, t] = jnp.full((1, LANES), -1.0, jnp.float32)

    for i in range(4):
        raw_copies[i].wait()
        for j in range(2):
            rows = pl.ds(i * 256 + j * 128, 128)
            values = raw[rows, :].astype(jnp.float32)
            squares = jnp.sum(values * values, axis=1, keepdims=True)
            unit[rows, :] = (values * lax.rsqrt(squares + 1e-06)).astype(jnp.bfloat16)

    tgt_copy.wait()
    target = tgt[...]
    row_block = target // ROWS
    t_core = row_block % 2
    t_group = row_block // (2 * BLOCKS) * 2 + t_core
    t_half = row_block // BLOCKS % 2
    t_place = row_block % BLOCKS // 2
    home = t_group * BLOCKS + block_at(t_half, t_place)
    slot_of = target % SLOT
    t_block = home % BLOCKS
    t_class = (t_group // 2 + t_block // 4 + t_block % 4) % 4
    position = (t_class * 32 + t_block * 2 + t_core) * SLOT + slot_of
    row_iota = lax.broadcasted_iota(jnp.int32, (PIECE, ROWS), 0)

    def permute(q):
        a = lax.rem(class_me + q, 4)
        onehot = jnp.where(row_iota == position - a * PIECE, 1.0, 0.0).astype(jnp.bfloat16)
        picked = jnp.dot(onehot, unit[...], preferred_element_type=jnp.float32)
        slots = PIECE // SLOT
        outgoing[pl.ds(a * slots, slots)] = picked.reshape(slots, SLOT, E).astype(jnp.bfloat16)

    routes = []
    for c in range(2):
        to_core = lax.rem(core + c, 2)
        sign = 2 * to_core - 1
        for dz in OFFSETS:
            for dy in OFFSETS:
                z, y = lax.rem(zme + dz, 4), lax.rem(yme + dy, 4)
                turn = lax.rem(z, 2)
                along = 1 - 2 * turn
                way = sign * along
                on_y = (y + way >= 0) & (y + way <= 3)
                on_z = (y == 3) & (way == 1)
                far_y = {0: way == 0, 1: way == -1, 2: way != 0, 3: way == 1}[dy]
                far_z = {0: turn == 2, 1: turn == 1, 2: turn != 2, 3: turn == 0}[dz]
                second = (on_y & far_y) | (on_z & far_z)
                block = z * 4 + y
                other = jnp.where(on_y, block + way, block + 4 * along)
                target = jnp.where(second, other, block)
                hop = (on_y & (lax.rem(target, 4) != yme)) | (on_z & (target // 4 != zme))
                which = jnp.where(second, NEAR, OWN)
                routes.append((c, dz, dy, block, (which, jnp.where(hop, 1, 0)), target))

    def send(q, c, x, home_block, which, block):
        to_core = core if c == 0 else 1 - core
        pltpu.make_async_remote_copy(
            outgoing.at[lax.rem(class_me + q, 4) * 32 + home_block * 2 + to_core],
            recv.at[which[0], class_me, zme, yme, core],
            a2a_ss,
            a2a_rs.at[which[0], 2 * q + c, which[1]],
            device_id=(2 * x + to_core, block),
            device_id_type=MESH,
        ).start()

    def send_known(q):
        for c, dz, dy, home_block, which, block in routes:
            if (dz + dy) % 4 != q:
                continue

            def go():
                send(q, c, xme, home_block, which, block)

            if c == 0:
                pl.when(block != bme)(go)
            else:
                go()

    def send_rest(q, dxs):
        for c, dz, dy, home_block, which, block in routes:
            dx = (q - dz - dy) % 4
            if dx:
                send(q, c, lax.rem(xme + dx, 4), home_block, which, block)

    def here(dx):
        pl.semaphore_wait(plane_sem.at[dx - 1], 1)

    permute(0)
    pl.semaphore_wait(barrier, 2 * BLOCKS - 1 + len(images))
    for dx, group in zip((2, 1, 3), images):
        pl.semaphore_signal(plane_sem.at[3 - dx], inc=1, device_id=(group, bme), device_id_type=MESH)
    for q in range(2):
        if q:
            permute(q)
        send_known(q)
    pltpu.make_async_copy(
        outgoing.at[class_me * 32 + bme * 2 + core],
        recv.at[OWN, class_me, zme, yme, core],
        a2a_rs.at[OWN, 0, 0],
    ).start()

    for dx in (1, 3, 2):
        here(dx)
    send_rest(0, ())
    send_rest(1, ())
    for q in range(2, STAGES):
        permute(q)
        send_known(q)
    send_rest(2, ())
    send_rest(3, ())

    @pl.when(has_from)
    def _():
        pltpu.make_async_copy(
            outgoing.at[lax.rem(sum_from, 4) * 32 + from_block * 2 + core],
            recv.at[NEAR, class_me, zme, yme, core],
            a2a_rs.at[NEAR, 2 * lax.rem(sum_from - sum_me + 4, 4), 0],
        ).start()

    for copy in lab_copies:
        copy.wait()
    stored = lax.broadcasted_iota(jnp.int32, (1, ROWS), 1)
    slot_no = stored // SLOT
    s_class, s_block, s_core = slot_no // 32, slot_no % 32 // 2, slot_no % 2
    s_x = (s_class - s_block // 4 - s_block % 4 + 8) % 4
    natural = ((2 * s_x + s_core) * BLOCKS + s_block) * SLOT + stored % SLOT
    lab_all = jnp.concatenate([lab_loc[i] for i in range(4)], axis=0)
    high = lab_all // 256
    halves = jnp.concatenate([high, lab_all - 256 * high], axis=0).astype(jnp.float32).astype(jnp.bfloat16)
    moved = jnp.zeros((8, ROWS), jnp.float32)
    for t in range(CHUNKS):
        move = jnp.where(row_iota[:LANES] == natural - t * LANES, 1.0, 0.0).astype(jnp.bfloat16)
        moved = moved + jnp.dot(
            halves[:, t * LANES : (t + 1) * LANES], move, preferred_element_type=jnp.float32
        )
    lab_new = moved[:4] * 256.0 + moved[4:]
    for i in range(4):
        lab_out[i] = lab_new[i : i + 1]

    lab_copy = pltpu.make_async_remote_copy(
        lab_out, lab_in, lab_ss, lab_rs, device_id=dev_sib, device_id_type=MESH
    )
    lab_copy.start()
    t_to, t_ok = partner(home % BLOCKS, t_core)
    dev_iota = lax.broadcasted_iota(jnp.int32, (DEVICES, ROWS), 0)
    devs = (home, t_group * BLOCKS + t_to, home + (1 - 2 * t_core) * BLOCKS)
    for which in range(3):
        picks[which] = jnp.where(dev_iota == devs[which], 1.0, 0.0).astype(jnp.bfloat16)

    lab_copy.wait()
    labels = [
        jnp.where(half == core, lab_out[i], lab_in[i]) for i in range(4)
    ]
    is0 = core == 0
    sides = [
        jnp.where(is0, labels[1], labels[2]),
        jnp.where(has_from, jnp.where(is0, labels[3], labels[0]), -2.0),
        jnp.where(is0, labels[2], labels[1]),
    ]
    for which in range(3):
        for t in range(CHUNKS):
            lane_lab[which, t] = sides[which][:, t * LANES : (t + 1) * LANES]

    four = recv.at[OWN, 0, 0, pl.ds(0, 2)]
    eight = recv.at[OWN, 0, 0]
    sixteen = recv.at[OWN, 0, pl.ds(0, 2)]
    thirty_two = recv.at[OWN, 0]

    def await_bytes(ref, sem):
        pltpu.make_async_copy(ref, ref, sem).wait()

    def hand_on(which, n, a, c, dy, dz, block, steps):
        for step in steps:
            await_bytes(four, a2a_rs.at[which, n, step])
            yy = lax.rem(yme + step * dy + 4, 4)
            zz = lax.rem(zme + step * dz + 4, 4)

            def go(src, dst):
                pltpu.make_async_remote_copy(
                    src, dst, rl_ss.at[which], rl_rs.at[1 - which, n], device_id=(gme, block), device_id_type=MESH
                ).start()

            @pl.when(dy != 0)
            def _():
                go(recv.at[which, a, :, yy, c], recv.at[1 - which, a, :, yy, c])

            @pl.when(dy == 0)
            def _():
                go(recv.at[which, a, zz, :, c], recv.at[1 - which, a, zz, :, c])

    def own_class(q):
        return lax.rem(sum_me - q + 4, 4)

    def near_class(q):
        return lax.rem(sum_from - q + 4, 4)

    def first(q, c):
        n = 2 * q + c
        from_core = lax.rem(core + c, 2)

        for step in range(2):

            @pl.when(has_to)
            def _():
                hand_on(OWN, n, own_class(q), from_core, yme - to_block % 4, zme - to_block // 4, to_block, (step,))

            @pl.when(has_from)
            def _():
                hand_on(
                    NEAR, n, near_class(q), from_core, yme - from_block % 4, zme - from_block // 4, from_block, (step,)
                )

        @pl.when(jnp.logical_not(has_to))
        def _():
            await_bytes(sixteen, a2a_rs.at[OWN, n, 0])

    def lay_out(which, x):
        got = recv[which, x].astype(jnp.float32)
        blk[which, pl.ds(x * PIECE, PIECE), :] = got.reshape(PIECE, E).astype(jnp.bfloat16)
        for c in range(2):
            col_lab[which, 2 * x + c] = lane_lab[which, 2 * x + c]

    r_iota = lax.broadcasted_iota(jnp.int32, (PIECE, LANES), 0)
    c_iota = lax.broadcasted_iota(jnp.int32, (PIECE, LANES), 1)
    ahead = r_iota - c_iota

    def product(a, x, b, same_block=False):
        gram = lax.dot_general(
            blk[a, pl.ds(x * PIECE, PIECE), :],
            blk[b],
            (((1,), (1,)), ((), ())),
            preferred_element_type=jnp.float32,
        )
        a_lab = jnp.concatenate(
            [jnp.broadcast_to(lane_lab[a, 2 * x + c], (LANES, LANES)).T for c in range(2)], axis=0
        )
        rows_best = jnp.full((PIECE, LANES), LOW, jnp.float32)
        for t in range(CHUNKS):
            cut = slice(t * LANES, (t + 1) * LANES)
            same = a_lab == col_lab[b, t]
            if same_block:
                same = same & (ahead != t * LANES - x * PIECE)
            masked = jnp.where(same, gram[:, cut], LOW)
            rows_best = jnp.maximum(rows_best, masked)
            col_best[b, :, cut] = jnp.maximum(
                col_best[b, :, cut], jnp.max(masked.reshape(PIECE // 8, 8, LANES), axis=0)
            )
        return rows_best

    def fold_rows(which, x, rows_best):
        for c in range(2):
            line = jnp.max(rows_best[c * LANES : (c + 1) * LANES].T, axis=0, keepdims=True)
            row_best[which, 2 * x + c] = jnp.maximum(row_best[which, 2 * x + c], line)

    def complete(q):
        x, w = own_class(q), near_class(q)

        @pl.when(has_to)
        def _():
            for c in range(2):
                await_bytes(eight, rl_rs.at[OWN, 2 * q + c])

        pltpu.make_async_remote_copy(
            recv.at[OWN, x], recv.at[SIB, x], sib_ss, sib_rs.at[q], device_id=dev_sib, device_id_type=MESH
        ).start()
        lay_out(OWN, x)

        @pl.when(has_from)
        def _():
            for c in range(2):
                await_bytes(eight, rl_rs.at[NEAR, 2 * q + c])
            lay_out(NEAR, w)

        own_rows = product(OWN, x, OWN, same_block=True)
        fold_rows(OWN, x, jnp.maximum(own_rows, product(OWN, x, NEAR)))
        fold_rows(NEAR, w, product(NEAR, w, OWN))

    third = 1 - core

    def sibling(q):
        x, w = own_class(q), near_class(q)
        await_bytes(thirty_two, sib_rs.at[q])
        lay_out(SIB, x)
        fold_rows(SIB, x, product(SIB, x, third))
        v = jnp.where(core == 0, w, x)
        fold_rows(third, v, product(third, v, SIB))

    def step(s, _):
        @pl.when(s < STAGES)
        def _():
            first(s, 0)
            first(s, 1)

        @pl.when(s >= 2)
        def _():
            sibling(s - 2)

        @pl.when((s >= 1) & (s < STAGES + 1))
        def _():
            complete(s - 1)

        return 0

    lax.fori_loop(0, STAGES + 2, step, 0, unroll=False)

    lines = []
    for which in range(3):
        cols = [
            jnp.max(col_best[which, :, t * LANES : (t + 1) * LANES], axis=0, keepdims=True)
            for t in range(CHUNKS)
        ]
        lines.append(jnp.maximum(jnp.concatenate(cols, axis=0), row_best[which][:, 0, :]))
    lane = lax.broadcasted_iota(jnp.int32, (CHUNKS, LANES), 1)
    for j in range(LANES // 16):
        own, near, sib = (
            pltpu.roll(line, (16 * which - 16 * j) % LANES, 1) for which, line in enumerate(lines)
        )
        packed = jnp.where(lane < 16, own, jnp.where(lane < 32, near, sib))
        for t in range(CHUNKS):
            score[j, t] = packed[t : t + 1]

    own_back = pltpu.make_async_copy(
        score.at[lax.rem(bme, 8), 2 * class_me + zme // 2], back.at[me], self_sem
    )
    own_back.start()

    order = sorted(
        ((dx, c, dz, dy) for dx in range(4) for c in range(2) for dz in range(4) for dy in range(4)),
        key=lambda o: -sum(min(d, 4 - d) for d in (o[0], o[2], o[3])),
    )
    zs = [lax.rem(zme + d, 4) for d in range(4)]
    ys = [lax.rem(yme + d, 4) for d in range(4)]
    gs = [[2 * lax.rem(xme + d, 4) + c for c in (core, 1 - core)] for d in range(4)]
    rows_at = [lax.rem(z, 2) * 4 for z in zs]
    for dx, c, dz, dy in order:
        if dx or c or dz or dy:
            z, y = zs[dz], ys[dy]
            pltpu.make_async_remote_copy(
                score.at[rows_at[dz] + y, 2 * lax.rem(sum_me + dx + dz + dy, 4) + z // 2],
                back.at[me],
                back_ss,
                back_rs,
                device_id=(gs[dx][c], z * 4 + y),
                device_id_type=MESH,
            ).start()

    await_bytes(outgoing.at[pl.ds(0, DEVICES - 2)], a2a_ss)

    @pl.when(jnp.logical_not(has_from))
    def _():
        await_bytes(outgoing.at[0], a2a_ss)

    @pl.when(has_to)
    def _():
        await_bytes(recv.at[OWN, pl.ds(0, 2)], rl_ss.at[OWN])

    @pl.when(has_from)
    def _():
        await_bytes(recv.at[OWN, pl.ds(0, 2)], rl_ss.at[NEAR])

    await_bytes(recv.at[OWN], sib_ss)
    own_back.wait()
    part = back.at[pl.ds(0, DEVICES - 1)]
    await_bytes(part, back_ss)
    await_bytes(part, back_rs)

    slot_iota = lax.broadcasted_iota(jnp.int32, (SLOT, ROWS), 0)
    best = jnp.full((SLOT, ROWS), LOW, jnp.float32)
    turned[...] = back[:, 0, :].T
    for which in range(3):
        rest = turned[pl.ds(16 * which + core * SLOT, SLOT), :]
        parts = []
        for _ in range(3):
            parts.append(rest.astype(jnp.bfloat16))
            rest = rest - parts[-1].astype(jnp.float32)
        slots = jnp.zeros((SLOT, ROWS), jnp.float32)
        for part in parts:
            slots = slots + jnp.dot(part, picks[which], preferred_element_type=jnp.float32)
        if which == NEAR:
            slots = jnp.where(t_ok, slots, LOW)
        best = jnp.maximum(best, slots)
    out[...] = jnp.sum(jnp.where(slot_iota == slot_of, best, 0.0), axis=0, keepdims=True)


def body(embeddings, target, cluster_labels):
    bf, f32, i32 = jnp.bfloat16, jnp.float32, jnp.int32
    dma = pltpu.SemaphoreType.DMA
    result = pl.pallas_call(
        kernel,
        out_shape=jax.ShapeDtypeStruct((1, ROWS), f32),
        in_specs=[pl.BlockSpec(memory_space=pl.ANY)] * 3,
        out_specs=pl.BlockSpec(memory_space=pltpu.VMEM),
        scratch_shapes=[
            pltpu.VMEM((ROWS, E), bf),
            pltpu.VMEM((ROWS, E), bf),
            pltpu.VMEM((DEVICES, SLOT, E), bf),
            pltpu.VMEM((3, 4, 4, 4, 2, SLOT, E), bf),
            pltpu.VMEM((3, ROWS, E), bf),
            pltpu.VMEM((1, ROWS), i32),
            pltpu.VMEM((4, 1, ROWS), i32),
            pltpu.VMEM((4, 1, ROWS), f32),
            pltpu.VMEM((4, 1, ROWS), f32),
            pltpu.VMEM((3, CHUNKS, 1, LANES), f32),
            pltpu.VMEM((3, CHUNKS, 1, LANES), f32),
            pltpu.VMEM((3, 8, ROWS), f32),
            pltpu.VMEM((3, CHUNKS, 1, LANES), f32),
            pltpu.VMEM((LANES // 16, CHUNKS, 1, LANES), f32),
            pltpu.VMEM((DEVICES, 1, LANES), f32),
            pltpu.VMEM((3, DEVICES, ROWS), bf),
            pltpu.VMEM((LANES, DEVICES), f32),
            dma((4,)),
            dma((4,)),
            dma,
            dma,
            dma, dma,
            dma, dma((2, GROUPS, 2)),
            dma((2,)), dma((2, GROUPS)),
            dma, dma((STAGES,)),
            dma, dma,
            pltpu.SemaphoreType.REGULAR((3,)),
        ],
        compiler_params=pltpu.CompilerParams(
            collective_id=0, has_side_effects=True, vmem_limit_bytes=60 * 2**20
        ),
        name="dedup_scores",
    )(embeddings, target.reshape(1, ROWS), cluster_labels.reshape(BLOCKS, 1, ROWS))
    return result.reshape(ROWS)


def solution(mesh):
    return jax.shard_map(
        body,
        mesh=mesh,
        in_specs=(P(("group", "block"), None), P(("group", "block")), P("group")),
        out_specs=P(("group", "block")),
        check_vma=False,
    )
```

```python
import jax
import jax.numpy as jnp
from jax import lax
from jax.experimental import pallas as pl
from jax.experimental.pallas import tpu as pltpu
from jax.sharding import PartitionSpec as P

MESH = pl.DeviceIdType.MESH
E = 1024
ROWS = 1024
GROUPS = 8
BLOCKS = 16
DEVICES = GROUPS * BLOCKS
SLOT = ROWS // DEVICES
LANES = 128
CHUNKS = ROWS // LANES
STAGES = 4
PIECE = ROWS // STAGES
LOW = -2.0
OWN, NEAR, SIB = 0, 1, 2
OFFSETS = (2, 1, 3, 0)


def place_of(block):
    z, y = block // 4, block % 4
    turn = z % 2
    return turn * 4 + y + turn * (3 - 2 * y)


def block_at(half, place):
    turn, r = place // 4, place % 4
    return (2 * half + turn) * 4 + r + turn * (3 - 2 * r)


def partner(block, core):
    place = place_of(block) - 1 + 2 * core
    ok = (place >= 0) & (place < 8)
    return block_at(block // 8, jnp.clip(place, 0, 7)), ok


def kernel(
    emb, tgt_hbm, lab, out,
    raw, unit, outgoing, recv, blk, tgt, lab_loc, lab_out, lab_in, lane_lab, col_lab, col_best, row_best, score, back, picks, turned,
    raw_sem, lab_sem, tgt_sem, self_sem, lab_ss, lab_rs, a2a_ss, a2a_rs, rl_ss, rl_rs, sib_ss, sib_rs,
    back_ss, back_rs, plane_sem,
):
    gme = lax.axis_index("group")
    bme = lax.axis_index("block")
    me = gme * BLOCKS + bme
    core = gme % 2
    gsib = gme + 1 - 2 * core
    xme, zme, yme = gme // 2, bme // 4, bme % 4
    place = place_of(bme)
    sum_me = xme + zme + yme
    half = bme // 8
    to_block, has_to = partner(bme, core)
    from_block, has_from = partner(bme, 1 - core)
    dev_sib = (gsib, bme)
    sum_from = xme + from_block // 4 + from_block % 4
    class_me = lax.rem(sum_me, 4)

    raw_copies = []
    for i in range(4):
        rows = pl.ds(i * 256, 256)
        raw_copies.append(pltpu.make_async_copy(emb.at[rows], raw.at[rows], raw_sem.at[i]))
    tgt_copy = pltpu.make_async_copy(tgt_hbm, tgt, tgt_sem)
    lab_copies = []
    for i in range(4):
        b = jnp.clip(2 * place - 1 + i, 0, BLOCKS - 1)
        lab_copies.append(pltpu.make_async_copy(lab.at[b], lab_loc.at[i], lab_sem.at[i]))
    for copy in raw_copies:
        copy.start()

    barrier = pltpu.get_barrier_semaphore()

    images = [2 * lax.rem(xme + dx, 4) + core for dx in (2, 1, 3)]

    offsets = sorted(
        ((dz, dy) for dz in range(4) for dy in range(4)), key=lambda o: -min(o[0], 4 - o[0]) - min(o[1], 4 - o[1])
    )
    peers = [
        (group, lax.rem(zme + dz, 4) * 4 + lax.rem(yme + dy, 4))
        for dz, dy in offsets
        for group in (gme, gsib)
    ][:-2]
    peers = peers[:10] + [(group, bme) for group in images] + peers[10:] + [dev_sib]
    for peer in peers:
        pl.semaphore_signal(barrier, inc=1, device_id=peer, device_id_type=MESH)
    for copy in [tgt_copy] + lab_copies:
        copy.start()

    for which in range(3):
        col_best[which] = jnp.full((8, ROWS), LOW, jnp.float32)
        for t in range(CHUNKS):
            row_best[which, t] = jnp.full((1, LANES), LOW, jnp.float32)
            col_lab[which, t] = jnp.full((1, LANES), -1.0, jnp.float32)

    for i in range(4):
        raw_copies[i].wait()
        for j in range(2):
            rows = pl.ds(i * 256 + j * 128, 128)
            values = raw[rows, :].astype(jnp.float32)
            squares = jnp.sum(values * values, axis=1, keepdims=True)
            unit[rows, :] = (values * lax.rsqrt(squares + 1e-06)).astype(jnp.bfloat16)

    tgt_copy.wait()
    target = tgt[...]
    row_block = target // ROWS
    t_core = row_block % 2
    t_group = row_block // (2 * BLOCKS) * 2 + t_core
    t_half = row_block // BLOCKS % 2
    t_place = row_block % BLOCKS // 2
    home = t_group * BLOCKS + block_at(t_half, t_place)
    slot_of = target % SLOT
    t_block = home % BLOCKS
    t_class = (t_group // 2 + t_block // 4 + t_block % 4) % 4
    position = (t_class * 32 + t_block * 2 + t_core) * SLOT + slot_of
    row_iota = lax.broadcasted_iota(jnp.int32, (PIECE, ROWS), 0)

    def permute(q):
        a = lax.rem(class_me + q, 4)
        onehot = jnp.where(row_iota == position - a * PIECE, 1.0, 0.0).astype(jnp.bfloat16)
        picked = jnp.dot(onehot, unit[...], preferred_element_type=jnp.float32)
        slots = PIECE // SLOT
        outgoing[pl.ds(a * slots, slots)] = picked.reshape(slots, SLOT, E).astype(jnp.bfloat16)

    routes = []
    for c in range(2):
        to_core = lax.rem(core + c, 2)
        sign = 2 * to_core - 1
        for dz in OFFSETS:
            for dy in OFFSETS:
                z, y = lax.rem(zme + dz, 4), lax.rem(yme + dy, 4)
                turn = lax.rem(z, 2)
                along = 1 - 2 * turn
                way = sign * along
                on_y = (y + way >= 0) & (y + way <= 3)
                on_z = (y == 3) & (way == 1)
                far_y = {0: way == 0, 1: way == -1, 2: way != 0, 3: way == 1}[dy]
                far_z = {0: turn == 2, 1: turn == 1, 2: turn != 2, 3: turn == 0}[dz]
                second = (on_y & far_y) | (on_z & far_z)
                block = z * 4 + y
                other = jnp.where(on_y, block + way, block + 4 * along)
                target = jnp.where(second, other, block)
                hop = (on_y & (lax.rem(target, 4) != yme)) | (on_z & (target // 4 != zme))
                which = jnp.where(second, NEAR, OWN)
                routes.append((c, dz, dy, block, (which, jnp.where(hop, 1, 0)), target))

    def send(q, c, x, home_block, which, block):
        to_core = core if c == 0 else 1 - core
        pltpu.make_async_remote_copy(
            outgoing.at[lax.rem(class_me + q, 4) * 32 + home_block * 2 + to_core],
            recv.at[which[0], class_me, zme, yme, core],
            a2a_ss,
            a2a_rs.at[which[0], 2 * q + c, which[1]],
            device_id=(2 * x + to_core, block),
            device_id_type=MESH,
        ).start()

    def send_known(q):
        for c, dz, dy, home_block, which, block in routes:
            if (dz + dy) % 4 != q:
                continue

            def go():
                send(q, c, xme, home_block, which, block)

            if c == 0:
                pl.when(block != bme)(go)
            else:
                go()

    def send_rest(q, dxs):
        for c, dz, dy, home_block, which, block in routes:
            dx = (q - dz - dy) % 4
            if dx:
                send(q, c, lax.rem(xme + dx, 4), home_block, which, block)

    def here(dx):
        pl.semaphore_wait(plane_sem.at[dx - 1], 1)

    permute(0)
    pl.semaphore_wait(barrier, 2 * BLOCKS - 1 + len(images))
    for dx, group in zip((2, 1, 3), images):
        pl.semaphore_signal(plane_sem.at[3 - dx], inc=1, device_id=(group, bme), device_id_type=MESH)
    for q in range(2):
        if q:
            permute(q)
        send_known(q)
    pltpu.make_async_copy(
        outgoing.at[class_me * 32 + bme * 2 + core],
        recv.at[OWN, class_me, zme, yme, core],
        a2a_rs.at[OWN, 0, 0],
    ).start()

    for dx in (1, 3, 2):
        here(dx)
    send_rest(0, ())
    send_rest(1, ())
    for q in range(2, STAGES):
        permute(q)
        send_known(q)
    send_rest(2, ())
    send_rest(3, ())

    @pl.when(has_from)
    def _():
        pltpu.make_async_copy(
            outgoing.at[lax.rem(sum_from, 4) * 32 + from_block * 2 + core],
            recv.at[NEAR, class_me, zme, yme, core],
            a2a_rs.at[NEAR, 2 * lax.rem(sum_from - sum_me + 4, 4), 0],
        ).start()

    for copy in lab_copies:
        copy.wait()
    stored = lax.broadcasted_iota(jnp.int32, (1, ROWS), 1)
    slot_no = stored // SLOT
    s_class, s_block, s_core = slot_no // 32, slot_no % 32 // 2, slot_no % 2
    s_x = (s_class - s_block // 4 - s_block % 4 + 8) % 4
    natural = ((2 * s_x + s_core) * BLOCKS + s_block) * SLOT + stored % SLOT
    lab_all = jnp.concatenate([lab_loc[i] for i in range(4)], axis=0)
    high = lab_all // 256
    halves = jnp.concatenate([high, lab_all - 256 * high], axis=0).astype(jnp.float32).astype(jnp.bfloat16)
    moved = jnp.zeros((8, ROWS), jnp.float32)
    for t in range(CHUNKS):
        move = jnp.where(row_iota[:LANES] == natural - t * LANES, 1.0, 0.0).astype(jnp.bfloat16)
        moved = moved + jnp.dot(
            halves[:, t * LANES : (t + 1) * LANES], move, preferred_element_type=jnp.float32
        )
    lab_new = moved[:4] * 256.0 + moved[4:]
    for i in range(4):
        lab_out[i] = lab_new[i : i + 1]

    lab_copy = pltpu.make_async_remote_copy(
        lab_out, lab_in, lab_ss, lab_rs, device_id=dev_sib, device_id_type=MESH
    )
    lab_copy.start()
    t_to, t_ok = partner(home % BLOCKS, t_core)
    dev_iota = lax.broadcasted_iota(jnp.int32, (DEVICES, ROWS), 0)
    devs = (home, t_group * BLOCKS + t_to, home + (1 - 2 * t_core) * BLOCKS)
    for which in range(3):
        picks[which] = jnp.where(dev_iota == devs[which], 1.0, 0.0).astype(jnp.bfloat16)

    lab_copy.wait()
    labels = [
        jnp.where(half == core, lab_out[i], lab_in[i]) for i in range(4)
    ]
    is0 = core == 0
    sides = [
        jnp.where(is0, labels[1], labels[2]),
        jnp.where(has_from, jnp.where(is0, labels[3], labels[0]), -2.0),
        jnp.where(is0, labels[2], labels[1]),
    ]
    for which in range(3):
        for t in range(CHUNKS):
            lane_lab[which, t] = sides[which][:, t * LANES : (t + 1) * LANES]

    four = recv.at[OWN, 0, 0, pl.ds(0, 2)]
    eight = recv.at[OWN, 0, 0]
    sixteen = recv.at[OWN, 0, pl.ds(0, 2)]
    thirty_two = recv.at[OWN, 0]

    def await_bytes(ref, sem):
        pltpu.make_async_copy(ref, ref, sem).wait()

    def hand_on(which, n, a, c, dy, dz, block, steps):
        for step in steps:
            await_bytes(four, a2a_rs.at[which, n, step])
            yy = lax.rem(yme + step * dy + 4, 4)
            zz = lax.rem(zme + step * dz + 4, 4)

            def go(src, dst):
                pltpu.make_async_remote_copy(
                    src, dst, rl_ss.at[which], rl_rs.at[1 - which, n], device_id=(gme, block), device_id_type=MESH
                ).start()

            @pl.when(dy != 0)
            def _():
                go(recv.at[which, a, :, yy, c], recv.at[1 - which, a, :, yy, c])

            @pl.when(dy == 0)
            def _():
                go(recv.at[which, a, zz, :, c], recv.at[1 - which, a, zz, :, c])

    def own_class(q):
        return lax.rem(sum_me - q + 4, 4)

    def near_class(q):
        return lax.rem(sum_from - q + 4, 4)

    def first(q, c):
        n = 2 * q + c
        from_core = lax.rem(core + c, 2)

        for step in range(2):

            @pl.when(has_to)
            def _():
                hand_on(OWN, n, own_class(q), from_core, yme - to_block % 4, zme - to_block // 4, to_block, (step,))

            @pl.when(has_from)
            def _():
                hand_on(
                    NEAR, n, near_class(q), from_core, yme - from_block % 4, zme - from_block // 4, from_block, (step,)
                )

        @pl.when(jnp.logical_not(has_to))
        def _():
            await_bytes(sixteen, a2a_rs.at[OWN, n, 0])

    def lay_out(which, x):
        got = recv[which, x].astype(jnp.float32)
        blk[which, pl.ds(x * PIECE, PIECE), :] = got.reshape(PIECE, E).astype(jnp.bfloat16)
        for c in range(2):
            col_lab[which, 2 * x + c] = lane_lab[which, 2 * x + c]

    r_iota = lax.broadcasted_iota(jnp.int32, (PIECE, LANES), 0)
    c_iota = lax.broadcasted_iota(jnp.int32, (PIECE, LANES), 1)
    ahead = r_iota - c_iota

    def product(a, x, b, same_block=False):
        gram = lax.dot_general(
            blk[a, pl.ds(x * PIECE, PIECE), :],
            blk[b],
            (((1,), (1,)), ((), ())),
            preferred_element_type=jnp.float32,
        )
        a_lab = jnp.concatenate(
            [jnp.broadcast_to(lane_lab[a, 2 * x + c], (LANES, LANES)).T for c in range(2)], axis=0
        )
        rows_best = jnp.full((PIECE, LANES), LOW, jnp.float32)
        for t in range(CHUNKS):
            cut = slice(t * LANES, (t + 1) * LANES)
            same = a_lab == col_lab[b, t]
            if same_block:
                same = same & (ahead != t * LANES - x * PIECE)
            masked = jnp.where(same, gram[:, cut], LOW)
            rows_best = jnp.maximum(rows_best, masked)
            col_best[b, :, cut] = jnp.maximum(
                col_best[b, :, cut], jnp.max(masked.reshape(PIECE // 8, 8, LANES), axis=0)
            )
        return rows_best

    def fold_rows(which, x, rows_best):
        for c in range(2):
            line = jnp.max(rows_best[c * LANES : (c + 1) * LANES].T, axis=0, keepdims=True)
            row_best[which, 2 * x + c] = jnp.maximum(row_best[which, 2 * x + c], line)

    def complete(q):
        x, w = own_class(q), near_class(q)

        @pl.when(has_to)
        def _():
            for c in range(2):
                await_bytes(eight, rl_rs.at[OWN, 2 * q + c])

        pltpu.make_async_remote_copy(
            recv.at[OWN, x], recv.at[SIB, x], sib_ss, sib_rs.at[q], device_id=dev_sib, device_id_type=MESH
        ).start()
        lay_out(OWN, x)

        @pl.when(has_from)
        def _():
            for c in range(2):
                await_bytes(eight, rl_rs.at[NEAR, 2 * q + c])
            lay_out(NEAR, w)

        own_rows = product(OWN, x, OWN, same_block=True)
        fold_rows(OWN, x, jnp.maximum(own_rows, product(OWN, x, NEAR)))
        fold_rows(NEAR, w, product(NEAR, w, OWN))

    third = 1 - core

    def sibling(q):
        x, w = own_class(q), near_class(q)
        await_bytes(thirty_two, sib_rs.at[q])
        lay_out(SIB, x)
        fold_rows(SIB, x, product(SIB, x, third))
        v = jnp.where(core == 0, w, x)
        fold_rows(third, v, product(third, v, SIB))

    def step(s, _):
        @pl.when(s < STAGES)
        def _():
            first(s, 0)
            first(s, 1)

        @pl.when(s >= 2)
        def _():
            sibling(s - 2)

        @pl.when((s >= 1) & (s < STAGES + 1))
        def _():
            complete(s - 1)

        return 0

    lax.fori_loop(0, STAGES + 2, step, 0, unroll=False)

    lines = []
    for which in range(3):
        cols = [
            jnp.max(col_best[which, :, t * LANES : (t + 1) * LANES], axis=0, keepdims=True)
            for t in range(CHUNKS)
        ]
        lines.append(jnp.maximum(jnp.concatenate(cols, axis=0), row_best[which][:, 0, :]))
    lane = lax.broadcasted_iota(jnp.int32, (CHUNKS, LANES), 1)
    for j in range(LANES // 16):
        own, near, sib = (
            pltpu.roll(line, (16 * which - 16 * j) % LANES, 1) for which, line in enumerate(lines)
        )
        packed = jnp.where(lane < 16, own, jnp.where(lane < 32, near, sib))
        for t in range(CHUNKS):
            score[j, t] = packed[t : t + 1]

    own_back = pltpu.make_async_copy(
        score.at[lax.rem(bme, 8), 2 * class_me + zme // 2], back.at[me], self_sem
    )
    own_back.start()

    order = sorted(
        ((dx, c, dz, dy) for dx in range(4) for c in range(2) for dz in range(4) for dy in range(4)),
        key=lambda o: -sum(min(d, 4 - d) for d in (o[0], o[2], o[3])),
    )
    zs = [lax.rem(zme + d, 4) for d in range(4)]
    ys = [lax.rem(yme + d, 4) for d in range(4)]
    gs = [[2 * lax.rem(xme + d, 4) + c for c in (core, 1 - core)] for d in range(4)]
    rows_at = [lax.rem(z, 2) * 4 for z in zs]
    for dx, c, dz, dy in order:
        if dx or c or dz or dy:
            z, y = zs[dz], ys[dy]
            pltpu.make_async_remote_copy(
                score.at[rows_at[dz] + y, 2 * lax.rem(sum_me + dx + dz + dy, 4) + z // 2],
                back.at[me],
                back_ss,
                back_rs,
                device_id=(gs[dx][c], z * 4 + y),
                device_id_type=MESH,
            ).start()

    await_bytes(outgoing.at[pl.ds(0, DEVICES - 2)], a2a_ss)

    @pl.when(jnp.logical_not(has_from))
    def _():
        await_bytes(outgoing.at[0], a2a_ss)

    @pl.when(has_to)
    def _():
        await_bytes(recv.at[OWN, pl.ds(0, 2)], rl_ss.at[OWN])

    @pl.when(has_from)
    def _():
        await_bytes(recv.at[OWN, pl.ds(0, 2)], rl_ss.at[NEAR])

    await_bytes(recv.at[OWN], sib_ss)
    own_back.wait()
    part = back.at[pl.ds(0, DEVICES - 1)]
    await_bytes(part, back_ss)
    await_bytes(part, back_rs)

    slot_iota = lax.broadcasted_iota(jnp.int32, (SLOT, ROWS), 0)
    best = jnp.full((SLOT, ROWS), LOW, jnp.float32)
    turned[...] = back[:, 0, :].T
    for which in range(3):
        rest = turned[pl.ds(16 * which + core * SLOT, SLOT), :]
        parts = []
        for _ in range(3):
            parts.append(rest.astype(jnp.bfloat16))
            rest = rest - parts[-1].astype(jnp.float32)
        slots = jnp.zeros((SLOT, ROWS), jnp.float32)
        for part in parts:
            slots = slots + jnp.dot(part, picks[which], preferred_element_type=jnp.float32)
        if which == NEAR:
            slots = jnp.where(t_ok, slots, LOW)
        best = jnp.maximum(best, slots)
    out[...] = jnp.sum(jnp.where(slot_iota == slot_of, best, 0.0), axis=0, keepdims=True)


def body(embeddings, target, cluster_labels):
    bf, f32, i32 = jnp.bfloat16, jnp.float32, jnp.int32
    dma = pltpu.SemaphoreType.DMA
    result = pl.pallas_call(
        kernel,
        out_shape=jax.ShapeDtypeStruct((1, ROWS), f32),
        in_specs=[pl.BlockSpec(memory_space=pl.ANY)] * 3,
        out_specs=pl.BlockSpec(memory_space=pltpu.VMEM),
        scratch_shapes=[
            pltpu.VMEM((ROWS, E), bf),
            pltpu.VMEM((ROWS, E), bf),
            pltpu.VMEM((DEVICES, SLOT, E), bf),
            pltpu.VMEM((3, 4, 4, 4, 2, SLOT, E), bf),
            pltpu.VMEM((3, ROWS, E), bf),
            pltpu.VMEM((1, ROWS), i32),
            pltpu.VMEM((4, 1, ROWS), i32),
            pltpu.VMEM((4, 1, ROWS), f32),
            pltpu.VMEM((4, 1, ROWS), f32),
            pltpu.VMEM((3, CHUNKS, 1, LANES), f32),
            pltpu.VMEM((3, CHUNKS, 1, LANES), f32),
            pltpu.VMEM((3, 8, ROWS), f32),
            pltpu.VMEM((3, CHUNKS, 1, LANES), f32),
            pltpu.VMEM((LANES // 16, CHUNKS, 1, LANES), f32),
            pltpu.VMEM((DEVICES, 1, LANES), f32),
            pltpu.VMEM((3, DEVICES, ROWS), bf),
            pltpu.VMEM((LANES, DEVICES), f32),
            dma((4,)),
            dma((4,)),
            dma,
            dma,
            dma, dma,
            dma, dma((2, GROUPS, 2)),
            dma((2,)), dma((2, GROUPS)),
            dma, dma((STAGES,)),
            dma, dma,
            pltpu.SemaphoreType.REGULAR((3,)),
        ],
        compiler_params=pltpu.CompilerParams(
            collective_id=0, has_side_effects=True, vmem_limit_bytes=60 * 2**20
        ),
        name="dedup_scores",
    )(embeddings, target.reshape(1, ROWS), cluster_labels.reshape(BLOCKS, 1, ROWS))
    return result.reshape(ROWS)


def solution(mesh):
    return jax.shard_map(
        body,
        mesh=mesh,
        in_specs=(P(("group", "block"), None), P(("group", "block")), P("group")),
        out_specs=P(("group", "block")),
        check_vma=False,
    )
```
